32 devices in a mesh: face: 4 (over y, x), tile: 8 (over z, core).
Axes of the slice: x: 2, y: 2, z: 4, core: 2. Of those that a mesh axis runs over, the one named last changes fastest.
Arguments:
- latlon: bfloat16 [2048, 74, 128], P(('face', 'tile')), may hold values from -6 to 6
- intersection_weight: bfloat16 [2048, 4, 128, 128], P(('face', 'tile')), may hold values from -0.5 to 0.5
- target_dev: int32 [2048, 4], P(('face', 'tile')), may hold values from 0 to 31, all different within a row; in each aligned block of 64 rows (0 to 63, 64 to 127, ...) at most 8 rows name the same one
- target_piece: int32 [2048, 4], P(('face', 'tile')), may hold values from 0 to 63
- counts: int32 [2048], P(('face', 'tile')), may hold values from 1 to 4
- conv_weight: bfloat16 [9, 256, 74], replicated, may hold values from -0.25 to 0.25
- cotangent: bfloat16 [4, 256, 128, 512], P('face', None, 'tile'), may hold values from -6 to 6
Outputs:
- activation: bfloat16 [4, 256, 128, 512], P('face', None, 'tile')
- grad_conv: float32 [9, 256, 74], replicated
- grad_latlon: bfloat16 [2048, 74, 128], P(('face', 'tile'))
The draws below stay inside these ranges and needn't reach their ends.
Inputs may be any that keep to these rules, and one draw needn't show every extreme that they name: `target_dev`: among the 4 entries of one block all owners differ; among the entries of one device's 64 blocks (aligned blocks of rows) no owner is named more than 8 times, a bound that some block reaches. Entries j >= counts[b] of block b are not live.
All inputs are finite; a program needn't handle non-finite values.
Results may differ from the reference program's by a relative error of at most 0.0091.
Values may be sent and summed in bfloat16 or wider, within the bound.
No kernel may reach another device: no remote copies, remote signals or barrier semaphores. Data moves between devices by JAX's collectives and lax.ppermute only.
A program may use at most 192 MiB of HBM per device.

```python
import math
import jax
import jax.numpy as jnp
import numpy as np
from jax import lax

C = 74
HID = 256
ROWS = 16
COLS = 512
PP = 128
BP = 128
K = 4
NB_DEV = 64
NB = 2048
PIECES = 64
CAP = 8
SIDE = 128
FACES = 4
N_FACE = 4
N_TILE = 8


def touch_ends(drawn, stream_key, least, high):
    longest = drawn.shape.index(max(drawn.shape))
    spots = []
    for shift in (0, 1):
        where = [jax.random.randint(jax.random.fold_in(stream_key, axis), (), 0, length) for axis, length in enumerate(drawn.shape)]
        where[longest] = (where[longest] + shift) % drawn.shape[longest]
        spots.append(tuple(where))
    return drawn.at[spots[0]].set(least).at[spots[1]].set(high)


def level_of(rng, dims, shards, low, top_value):
    def one(position, blocks):
        heights = jax.random.uniform(jax.random.fold_in(jax.random.fold_in(rng, 6), position), (blocks,), jnp.float32, low / len(shards), top_value / len(shards))
        return jnp.repeat(jnp.exp(heights), dims[position] // blocks).reshape((-1,) + (1,) * (len(dims) - position - 1))

    gain = one(*shards[0])
    for cut in shards[1:]:
        gain = gain * one(*cut)
    return gain


def shared_out(rng, own, number, rows, count, top, limit, skew):
    ranking = jax.random.permutation(rng, count)
    packed, ordinary = load_shares(count, rows * top, limit, skew, True), load_shares(count, rows * top, limit, skew, False)
    places = jnp.arange(count)

    def named(tallies, turn):
        used = int((tallies > 0).sum())
        fixed = max(1, used // 4)
        passed = fixed + (places - fixed + turn * (used - fixed)) % max(1, count - fixed)
        return jnp.zeros((count,), jnp.int32).at[ranking[jnp.where(places < fixed, places, passed)]].set(jnp.asarray(tallies, jnp.int32))

    tallies = jnp.where(number % 4 == 0, named(packed, number // 4), named(ordinary, number - number // 4 - 1))
    mixed = jax.random.permutation(jax.random.fold_in(own, 3), count)
    source_of, receiver = mixed[0:count // 2 * 2:2], mixed[1:count // 2 * 2:2]
    slack = jnp.minimum(tallies[source_of] - 1, limit - tallies[receiver]) // 2
    slack = jnp.where((source_of == ranking[0]) | (receiver == ranking[0]) | (tallies[receiver] == 0), 0, jnp.maximum(slack, 0))
    passed = jax.random.randint(jax.random.fold_in(own, 4), (count // 2,), 0, 1 << 20) % (slack + 1)
    tallies = tallies.at[source_of].add(-passed).at[receiver].add(passed)
    items = jnp.searchsorted(jnp.cumsum(tallies), jnp.arange(rows * top), side="right").astype(jnp.int32)
    grid = items.reshape(top, rows).T
    grid = grid[jax.random.permutation(jax.random.fold_in(own, 1), rows)]
    turn = jax.random.randint(jax.random.fold_in(own, 2), (rows, 1), 0, top)
    return jnp.take_along_axis(grid, (jnp.arange(top)[None, :] + turn) % top, axis=1)


def load_shares(number_of, total, most, lean, full):
    portions = [(1 << 20) // math.isqrt(rank ** lean) + 1 for rank in range(1, number_of + 1)]
    largest = most if full else min(most, max(-(-total // number_of), total * portions[0] // sum(portions)))
    least = 1 if total - largest >= number_of - 1 else 0
    given, spare = [largest] + [least] * (number_of - 1), total - largest - least * (number_of - 1)
    while spare > 0:
        candidates = [i for i in range(1, number_of) if given[i] < largest] or [i for i in range(1, number_of) if given[i] < most]
        mass, left = sum([portions[i] for i in candidates]), spare
        for i in candidates:
            more = min(most - given[i], max(1, left * portions[i] // mass), spare)
            given[i] = given[i] + more
            spare = spare - more
    return np.array(given)


def noise(own_key, extent, scale, most, cuts=(), kind=jnp.bfloat16):
    drawn = jax.random.normal(own_key, extent, jnp.float32) * scale
    if len(cuts) > 0:
        drawn = level_of(own_key, extent, cuts, -0.22, 0.18) * drawn
    return jnp.clip(drawn, min=-most, max=most).astype(kind)


def setup_inputs(seed: int = 0) -> dict:
    key_list = jax.random.split(jax.random.key(seed), 8)
    latlon = noise(key_list[0], (NB, C, BP), 1.0, 6.0, ((0, 32),))
    intersection_weight = noise(key_list[1], (NB, K, BP, PP), BP ** -0.5, 0.5, ((0, 32),))
    target_dev_keys = jax.random.split(jax.random.fold_in(key_list[2], 1), NB // NB_DEV)
    target_dev_turns = jax.random.permutation(jax.random.fold_in(key_list[2], 3), NB // NB_DEV)
    target_dev = jax.vmap(lambda own, number: shared_out(jax.random.fold_in(key_list[2], 2), own, number, NB_DEV, N_FACE * N_TILE, K, CAP, 2))(target_dev_keys, target_dev_turns).reshape((NB, K))
    target_piece = touch_ends(jax.random.randint(key_list[3], (NB, K), 0, PIECES), jax.random.fold_in(key_list[3], 1), 0, PIECES - 1).astype(jnp.int32)
    counts = touch_ends(jax.random.randint(key_list[4], (NB,), 1, K + 1), jax.random.fold_in(key_list[4], 1), 1, K).astype(jnp.int32)
    conv_weight = noise(key_list[5], (9, HID, C), (9 * C) ** -0.5, 0.25)
    cotangent = noise(key_list[6], (FACES, HID, SIDE, COLS), 1.0, 6.0, ((0, 4), (2, 8)))
    return dict(latlon=latlon, intersection_weight=intersection_weight, target_dev=target_dev, target_piece=target_piece, counts=counts, conv_weight=conv_weight, cotangent=cotangent)


def gelu_parts(value):
    inner = 0.7978845608 * (value + 0.044715 * value * value * value)
    tanh_part = jnp.tanh(inner)
    result = 0.5 * value * (1.0 + tanh_part)
    slope = 0.5 * (1.0 + tanh_part) + 0.5 * value * (1.0 - tanh_part * tanh_part) * 0.7978845608 * (1.0 + 0.134145 * value * value)
    return (result, slope)

def cycle_pad(array):
    padded = jnp.pad(array, ((0, 0), (1, 1), (0, 0)))
    return jnp.concatenate([padded[:, :, -1:], padded, padded[:, :, :1]], axis=2)

def to_cycle(array):
    return array.transpose(1, 2, 0, 3).reshape(array.shape[1], array.shape[2], array.shape[0] * array.shape[3])

def from_cycle(array):
    return array.reshape(array.shape[0], array.shape[1], N_FACE, COLS).transpose(2, 0, 1, 3)

def reference(latlon, intersection_weight, target_dev, target_piece, counts, conv_weight, cotangent):
    devices = N_FACE * N_TILE
    blocks = latlon.shape[0] // devices
    live = (jnp.arange(K, dtype=jnp.int32)[None, :] < counts[:, None]).astype(jnp.float32)
    dest = (target_dev * PIECES + target_piece).astype(jnp.int32)
    groups = (latlon.reshape(devices, blocks, C, BP), intersection_weight.reshape(devices, blocks, K, BP, PP), dest.reshape(devices, blocks, K), live.reshape(devices, blocks, K))

    def regrid(field_sum, items):
        lat, weights, targets, alive = items
        part = jnp.einsum('bcp,bjpq->bjcq', lat.astype(jnp.float32), weights.astype(jnp.float32)) * alive[:, :, None, None]
        part = lax.optimization_barrier(part.astype(jnp.bfloat16)).astype(jnp.float32)
        field_sum = field_sum.at[targets.reshape(-1)].add(part.reshape(-1, C, PP))
        return (field_sum, None)
    field_sum, unused = lax.scan(regrid, jnp.zeros((devices * PIECES, C, PP), jnp.float32), groups)
    field = field_sum.astype(jnp.bfloat16).reshape(N_FACE, N_TILE, PIECES, C, PP).transpose(0, 3, 1, 2, 4)
    field = field.reshape(N_FACE, C, N_TILE * ROWS, COLS)
    cycle = N_FACE * COLS
    field_pad = cycle_pad(to_cycle(field))
    cot_cycle = to_cycle(cotangent)
    kernel = conv_weight.astype(jnp.float32)

    def band(grad_sum, tile):
        window = lax.dynamic_slice_in_dim(field_pad, tile * ROWS, ROWS + 2, axis=1).astype(jnp.float32)
        cot = lax.dynamic_slice_in_dim(cot_cycle, tile * ROWS, ROWS, axis=1).astype(jnp.float32)
        pre = jnp.zeros((HID, ROWS, cycle), jnp.float32)
        for k in range(9):
            ky, kx = divmod(k, 3)
            pre = pre + jnp.einsum('oc,crw->orw', kernel[k], window[:, ky:ky + ROWS, kx:kx + cycle])
        result, slope = gelu_parts(pre)
        dpre = (cot * slope).astype(jnp.bfloat16)
        dpre_f = lax.optimization_barrier(dpre).astype(jnp.float32)
        terms = []
        for k in range(9):
            ky, kx = divmod(k, 3)
            terms.append(jnp.einsum('orw,crw->oc', dpre_f, window[:, ky:ky + ROWS, kx:kx + cycle]))
        return (grad_sum + jnp.stack(terms), (result.astype(jnp.bfloat16), dpre))
    grad_sum, outs = lax.scan(band, jnp.zeros((9, HID, C), jnp.float32), jnp.arange(N_TILE, dtype=jnp.int32))
    act_bands, dpre_bands = outs
    activation = from_cycle(act_bands.transpose(1, 0, 2, 3).reshape(HID, N_TILE * ROWS, cycle))
    dpre_pad = cycle_pad(dpre_bands.transpose(1, 0, 2, 3).reshape(HID, N_TILE * ROWS, cycle))

    def back(carry, tile):
        window = lax.dynamic_slice_in_dim(dpre_pad, tile * ROWS, ROWS + 2, axis=1).astype(jnp.float32)
        total = jnp.zeros((C, ROWS, cycle), jnp.float32)
        for k in range(9):
            ky, kx = divmod(k, 3)
            total = total + jnp.einsum('oc,orw->crw', kernel[k], window[:, 2 - ky:2 - ky + ROWS, 2 - kx:2 - kx + cycle])
        return (carry, total.astype(jnp.bfloat16))
    unused, dbands = lax.scan(back, jnp.zeros((), jnp.float32), jnp.arange(N_TILE, dtype=jnp.int32))
    dfield = from_cycle(dbands.transpose(1, 0, 2, 3).reshape(C, N_TILE * ROWS, cycle))
    dfield = dfield.reshape(N_FACE, C, N_TILE, ROWS * COLS).transpose(0, 2, 1, 3)
    dfield = dfield.reshape(devices, C, PIECES, PP).transpose(0, 2, 1, 3).reshape(devices * PIECES, C, PP)

    def unregrid(carry, items):
        lat, weights, targets, alive = items
        got = dfield[targets].astype(jnp.float32) * alive[:, :, None, None]
        grad = jnp.einsum('bjcq,bjpq->bcp', got, weights.astype(jnp.float32))
        return (carry, grad.astype(jnp.bfloat16))
    unused, grad_lat = lax.scan(unregrid, jnp.zeros((), jnp.float32), groups)
    grad_latlon = grad_lat.reshape(devices * blocks, C, BP)
    grad_conv = grad_sum * (1.0 / math.sqrt(N_FACE * N_TILE * ROWS * COLS))
    return (activation, grad_conv, grad_latlon)
```

```python
import functools
import math

import jax
import jax.numpy as jnp
from jax import lax
from jax.experimental import pallas as pl
from jax.experimental.pallas import tpu as pltpu
from jax.sharding import PartitionSpec as P

C = 74
CP = 80
HID = 256
ROWS = 16
COLS = 512
PP = 128
K = 4
PIECES = 64
TILE = 16
BOTH = ("face", "tile")
VMEM_LIMIT = 58 * 1024 * 1024
F32 = jnp.float32
BF16 = jnp.bfloat16


def params():
    return pltpu.CompilerParams(vmem_limit_bytes=VMEM_LIMIT)


def whole(shape):
    return pl.BlockSpec(shape, lambda *_: (0,) * len(shape))


def smem():
    return pl.BlockSpec(memory_space=pltpu.SMEM)


def send_kernel(
    slots, part, group, dev_ref, piece_ref, counts_ref, lat_ref, weight_ref, send_ref, place_ref, lat_f, store, packed, tally, sem
):
    step = pl.program_id(0)
    blocks = lat_ref.shape[1]
    devices = send_ref.shape[0] // part
    trash = devices * part
    codes = part - TILE

    @pl.when(step == 0)
    def _():
        def clear(d, carry):
            tally[d] = 0
            at = pl.multiple_of(d * part, TILE)
            store[pl.ds(at, codes), :] = jnp.zeros((codes, PP), F32)
            store[pl.ds(at + codes, TILE), :] = jnp.full((TILE, PP), -1.0, F32)
            return carry

        lax.fori_loop(0, devices, clear, 0)
        for c in range(C):
            lat_f[c * blocks : (c + 1) * blocks, :] = lat_ref[c].astype(F32)

    for i in range(group):
        b = step * group + i
        rows = lat_f[pl.ds(b, C, stride=blocks), :].astype(BF16)
        for half in range(2):
            pair = jnp.concatenate([weight_ref[i, 2 * half], weight_ref[i, 2 * half + 1]], axis=1)
            product = jnp.dot(rows, pair, preferred_element_type=F32)
            for part_j in range(2):
                j = 2 * half + part_j
                live = j < counts_ref[b]
                d = dev_ref[b, j]
                s = tally[d]
                tally[d] = s + live.astype(jnp.int32)
                at = jnp.where(live, d * part + s, trash)
                place_ref[b * K + j] = jnp.where(live, d * (part - TILE) + s, -1)
                store[pl.ds(at, C, stride=slots), :] = product[:, part_j * PP : (part_j + 1) * PP]
                at_code = jnp.where(live, d * part + codes + s, trash)
                code = jnp.full((TILE // slots, PP), piece_ref[b, j].astype(F32), F32)
                store[pl.ds(at_code, TILE // slots, stride=slots), :] = code

    @pl.when(step == pl.num_programs(0) - 1)
    def _():
        quarter = devices // 4 * part

        def ship(k):
            return pltpu.make_async_copy(
                packed.at[pl.ds(k * quarter, quarter)], send_ref.at[pl.ds(k * quarter, quarter)], sem.at[k]
            )

        for k in range(4):

            def pack(d, carry):
                at = pl.multiple_of(k * quarter + d * part, TILE)
                packed[pl.ds(at, part), :] = store[pl.ds(at, part), :].astype(BF16)
                return carry

            lax.fori_loop(0, devices // 4, pack, 0)
            ship(k).start()
        for k in range(4):
            ship(k).wait()


def send_call(dev, piece, counts, lat, weights, devices, slots, part):
    blocks = lat.shape[1]
    group = 8
    return pl.pallas_call(
        functools.partial(send_kernel, slots, part, group),
        grid=(blocks // group,),
        in_specs=[
            smem(),
            smem(),
            smem(),
            whole(lat.shape),
            pl.BlockSpec((group, K, PP, PP), lambda g: (g, 0, 0, 0)),
        ],
        out_specs=[pl.BlockSpec(memory_space=pl.ANY), smem()],
        out_shape=[
            jax.ShapeDtypeStruct((devices * part, PP), BF16),
            jax.ShapeDtypeStruct((blocks * K,), jnp.int32),
        ],
        scratch_shapes=[
            pltpu.VMEM((CP * blocks, PP), F32),
            pltpu.VMEM((devices * part + CP * slots + 8, PP), F32),
            pltpu.VMEM((devices * part, PP), BF16),
            pltpu.SMEM((devices,), jnp.int32),
            pltpu.SemaphoreType.DMA((4,)),
        ],
        compiler_params=params(),
        name="block_products",
    )(dev, piece, counts, lat, weights)


def lane_of(shape):
    return lax.broadcasted_iota(jnp.int32, shape, 1)


def put_columns(message, row, lane, first, second):
    message = jnp.where(lane == row, first, message)
    return jnp.where(lane == 32 + row, second, message)


def gather_kernel(slots, recv_ref, field_ref, low_ref, high_ref, west_ref, east_ref, pick_ref, total):
    devices, part = recv_ref.shape[0], recv_ref.shape[1]
    per = TILE // slots
    tiles = part // TILE - 1
    keys = devices * TILE
    codes = recv_ref[:, part - TILE :, :].astype(F32).reshape(keys, PP).astype(jnp.int32)
    within = lax.rem(lax.broadcasted_iota(jnp.int32, (keys, PP), 0), TILE)
    codes = jnp.where(codes < 0, -4096, codes + within // slots * PIECES)
    wide = per * PIECES
    picks = []
    for t in range(wide // PP):
        picks.append((codes == lane_of((keys, PP)) + t * PP).astype(F32))
    pick = jnp.concatenate(picks, axis=1) if len(picks) > 1 else picks[0]
    pick_ref[...] = pick.astype(BF16)
    pick_t = jnp.transpose(pick).astype(BF16)
    total[...] = jnp.zeros(total.shape, F32)
    for t in range(0, tiles, 2):
        pair = [t, t + 1] if t + 1 < tiles else [t]
        data = [recv_ref[:, u * TILE : (u + 1) * TILE, :].reshape(keys, PP) for u in pair]
        data = jnp.concatenate(data, axis=1) if len(data) > 1 else data[0]
        sums = jnp.dot(pick_t, data, preferred_element_type=F32)
        for n, u in enumerate(pair):
            for p in range(per):
                c = u * per + p
                if c < C:
                    total[pl.ds(c, PIECES, stride=CP), :] = sums[
                        p * PIECES : (p + 1) * PIECES, n * PP : (n + 1) * PP
                    ]
    lane = lane_of((CP, PP))
    west = jnp.zeros((CP, PP), F32)
    east = jnp.zeros((CP, PP), F32)
    quarters = COLS // PP
    for r in range(ROWS):
        for q in range(quarters):
            piece = r * quarters + q
            block = total[piece * CP : (piece + 1) * CP, :]
            out = block.astype(BF16)
            field_ref[r, :, q * PP : (q + 1) * PP] = out
            if r < 2:
                low_ref[r, :, q * PP : (q + 1) * PP] = out
            if r >= ROWS - 2:
                high_ref[r - ROWS + 2, :, q * PP : (q + 1) * PP] = out
            if q == 0:
                west = put_columns(west, r + 2, lane, block[:, 0:1], block[:, 1:2])
            if q == quarters - 1:
                east = put_columns(east, r + 2, lane, block[:, PP - 2 : PP - 1], block[:, PP - 1 : PP])
    west_ref[...] = west.astype(BF16)
    east_ref[...] = east.astype(BF16)


def gather_call(recv, slots):
    devices = recv.shape[0]
    wide = TILE // slots * PIECES
    shapes = [(ROWS, CP, COLS), (2, CP, COLS), (2, CP, COLS), (CP, PP), (CP, PP), (devices * TILE, wide)]
    return pl.pallas_call(
        functools.partial(gather_kernel, slots),
        grid=(1,),
        in_specs=[whole(recv.shape)],
        out_specs=[whole(s) for s in shapes],
        out_shape=[jax.ShapeDtypeStruct(s, BF16) for s in shapes],
        scratch_shapes=[pltpu.VMEM((PIECES * CP, PP), F32)],
        compiler_params=params(),
        name="field_sum",
    )(recv)


def columns_kernel(west0, east0, top_ref, bottom_ref, west_ref, east_ref):
    lane = lane_of((CP, PP))
    west = west0[...].astype(F32)
    east = east0[...].astype(F32)
    for row, ref, i in ((0, top_ref, 0), (1, top_ref, 1), (ROWS + 2, bottom_ref, 0), (ROWS + 3, bottom_ref, 1)):
        left = ref[i, :, 0:PP].astype(F32)
        right = ref[i, :, COLS - PP : COLS].astype(F32)
        west = put_columns(west, row, lane, left[:, 0:1], left[:, 1:2])
        east = put_columns(east, row, lane, right[:, PP - 2 : PP - 1], right[:, PP - 1 : PP])
    west_ref[...] = west.astype(BF16)
    east_ref[...] = east.astype(BF16)


def columns_call(west, east, top, bottom):
    return pl.pallas_call(
        columns_kernel,
        out_shape=[jax.ShapeDtypeStruct((CP, PP), BF16)] * 2,
        name="edge_columns",
    )(west, east, top, bottom)


def gelu_parts(value):
    square = value * value
    tanh_part = jnp.tanh(value * (0.7978845608 + (0.7978845608 * 0.044715) * square))
    half = 0.5 + 0.5 * tanh_part
    inner = (0.5 * 0.7978845608) + (0.5 * 0.7978845608 * 0.134145) * square
    slope = half + value * inner * (1.0 - tanh_part * tanh_part)
    return (value * half, slope)


def conv_kernel(
    slots,
    field_ref,
    top_ref,
    bottom_ref,
    own_west,
    own_east,
    far_west,
    far_east,
    cot_ref,
    cot_top,
    cot_bottom,
    cot_cols,
    forward_ref,
    backward_ref,
    pick_ref,
    act_ref,
    grad_ref,
    reply_ref,
    stack,
    dpre,
    side,
    dfield,
    packed,
    sem,
):
    step = pl.program_id(0)
    last = ROWS + 1
    lane = lane_of((CP, PP))
    lane_wide = lane_of((CP, COLS))

    def column(ref, at):
        return jnp.sum(jnp.where(lane == at, ref[...].astype(F32), 0.0), axis=1, keepdims=True)

    def build(row, rows):
        before = column(far_west, 32 + row)
        after = column(far_east, row)
        middle = rows.astype(F32)
        left = jnp.where(lane_wide == 0, before, pltpu.roll(middle, 1, 1))
        right = jnp.where(lane_wide == COLS - 1, after, pltpu.roll(middle, COLS - 1, 1))
        stack[row, 0:CP, :] = left.astype(BF16)
        stack[row, CP : 2 * CP, :] = rows
        stack[row, 2 * CP : 3 * CP, :] = right.astype(BF16)

    @pl.when(step == 0)
    def _():
        build(0, top_ref[0])
        build(1, top_ref[1])
        build(2, field_ref[0])
        grad_ref[...] = jnp.zeros(grad_ref.shape, F32)
        wests = [far_west[...].astype(F32)] * 2 + [own_west[...].astype(F32)]
        easts = [own_east[...].astype(F32)] + [far_east[...].astype(F32)] * 2
        west_at = (0, 32, 0)
        east_at = (32, 0, 32)
        pre = jnp.zeros((HID, PP), F32)
        for ky in range(3):
            parts = []
            for kx in range(3):
                w = pltpu.roll(wests[kx], (2 * PP - west_at[kx] - ky) % PP, 1)
                e = pltpu.roll(easts[kx], (2 * PP + 64 - east_at[kx] - ky) % PP, 1)
                parts.append(jnp.where(lane < 64, w, e))
            columns = jnp.concatenate(parts, axis=0).astype(BF16)
            pre = pre + jnp.dot(forward_ref[ky], columns, preferred_element_type=F32)
        unused, slope = gelu_parts(pre)
        dcol = (cot_cols[...].astype(F32) * slope).astype(BF16).astype(F32)
        sums = jnp.zeros((3 * CP, PP), F32)
        for ky in range(3):
            moved = pltpu.roll(dcol, (PP - (2 - ky)) % PP, 1).astype(BF16)
            sums = sums + jnp.dot(backward_ref[ky], moved, preferred_element_type=F32)
        side[...] = sums

    @pl.when(step <= last)
    def _():
        for n in range(2):
            cols = slice(n * 256, (n + 1) * 256)
            pre = jnp.dot(forward_ref[0], stack[step, :, cols], preferred_element_type=F32)
            pre = pre + jnp.dot(forward_ref[1], stack[step + 1, :, cols], preferred_element_type=F32)
            pre = pre + jnp.dot(forward_ref[2], stack[step + 2, :, cols], preferred_element_type=F32)
            result, slope = gelu_parts(pre)
            cot = jnp.where(
                step == 0, cot_top[:, cols], jnp.where(step == last, cot_bottom[:, cols], cot_ref[0, :, cols])
            )
            dpre[step, :, cols] = (cot.astype(F32) * slope).astype(BF16)

            @pl.when(step < last)
            def _():
                act_ref[0, :, cols] = result.astype(BF16)

    @pl.when(step <= ROWS - 2)
    def _():
        build(step + 3, field_ref[jnp.minimum(step + 1, ROWS - 1)])

    @pl.when(step == ROWS - 1)
    def _():
        build(ROWS + 2, bottom_ref[0])

    @pl.when(step == ROWS)
    def _():
        build(ROWS + 3, bottom_ref[1])

    @pl.when((step >= 3) & (step <= ROWS + 2))
    def _():
        r = step - 3
        own = dpre[r + 1]
        for ky in range(3):
            grad_ref[ky] += lax.dot_general(
                stack[r + 1 + ky], own, (((1,), (1,)), ((), ())), preferred_element_type=F32
            )
        out = jnp.dot(backward_ref[0], dpre[r + 2], preferred_element_type=F32)
        out = out + jnp.dot(backward_ref[1], own, preferred_element_type=F32)
        out = out + jnp.dot(backward_ref[2], dpre[r], preferred_element_type=F32)
        after = jnp.sum(jnp.where(lane == 64 + r, side[0:CP, :], 0.0), axis=1, keepdims=True)
        before = jnp.sum(jnp.where(lane == r, side[2 * CP :, :], 0.0), axis=1, keepdims=True)
        rows = (
            jnp.where(lane_wide == COLS - 1, after, pltpu.roll(out[0:CP], COLS - 1, 1))
            + out[CP : 2 * CP]
            + jnp.where(lane_wide == 0, before, pltpu.roll(out[2 * CP :], 1, 1))
        )
        quarters = COLS // PP
        for q in range(quarters):
            at = pl.multiple_of((r * quarters + q) * CP, 8)
            dfield[pl.ds(at, CP), :] = rows[:, q * PP : (q + 1) * PP]

    @pl.when(step == ROWS + 2)
    def _():
        devices = packed.shape[0]
        per = TILE // slots
        tiles = packed.shape[1] // TILE
        middle = tiles // 4 * 2
        pick = pick_ref[...]

        def ship(k):
            rows = pl.ds(0, middle * TILE) if k == 0 else pl.ds(middle * TILE, (tiles - middle) * TILE)
            return pltpu.make_async_copy(packed.at[:, rows, :], reply_ref.at[:, rows, :], sem.at[k])

        for t in range(0, tiles, 2):
            pair = [t, t + 1] if t + 1 < tiles else [t]
            data = []
            for u in pair:
                chans = [
                    dfield[pl.ds(min(u * per + p, CP - 1), PIECES, stride=CP), :].astype(BF16) for p in range(per)
                ]
                data.append(jnp.concatenate(chans, axis=0) if per > 1 else chans[0])
            data = jnp.concatenate(data, axis=1) if len(data) > 1 else data[0]
            got = jnp.dot(pick, data, preferred_element_type=F32).astype(BF16)
            for n, u in enumerate(pair):
                packed[:, u * TILE : (u + 1) * TILE, :] = got[:, n * PP : (n + 1) * PP].reshape(devices, TILE, PP)
            if t + 2 == middle:
                ship(0).start()
        ship(1).start()
        ship(0).wait()
        ship(1).wait()


def conv_call(slots, part, field, top, bottom, own_west, own_east, far_west, far_east, cot, cot_top, cot_bottom, cot_cols, forward, backward, pick):
    devices = pick.shape[0] // TILE

    def row(s):
        return (jnp.clip(s - 1, 0, ROWS - 1), 0, 0)

    reply_rows = part - TILE
    return pl.pallas_call(
        functools.partial(conv_kernel, slots),
        grid=(ROWS + 3,),
        in_specs=[
            whole(field.shape),
            whole(top.shape),
            whole(bottom.shape),
            whole(own_west.shape),
            whole(own_east.shape),
            whole(far_west.shape),
            whole(far_east.shape),
            pl.BlockSpec((1, HID, COLS), row),
            whole(cot_top.shape),
            whole(cot_bottom.shape),
            whole(cot_cols.shape),
            whole(forward.shape),
            whole(backward.shape),
            whole(pick.shape),
        ],
        out_specs=[
            pl.BlockSpec((1, HID, COLS), row),
            whole((3, 3 * CP, HID)),
            pl.BlockSpec(memory_space=pl.ANY),
        ],
        out_shape=[
            jax.ShapeDtypeStruct((ROWS, HID, COLS), BF16),
            jax.ShapeDtypeStruct((3, 3 * CP, HID), F32),
            jax.ShapeDtypeStruct((devices, reply_rows, PP), BF16),
        ],
        scratch_shapes=[
            pltpu.VMEM((ROWS + 4, 3 * CP, COLS), BF16),
            pltpu.VMEM((ROWS + 2, HID, COLS), BF16),
            pltpu.VMEM((3 * CP, PP), F32),
            pltpu.VMEM((PIECES * CP, PP), F32),
            pltpu.VMEM((devices, reply_rows, PP), BF16),
            pltpu.SemaphoreType.DMA((2,)),
        ],
        compiler_params=params(),
        name="conv_level",
    )(field, top, bottom, own_west, own_east, far_west, far_east, cot, cot_top, cot_bottom, cot_cols, forward, backward, pick)


def return_kernel(slots, group, place_ref, back_ref, weight_ref, out_ref, back_f, out_f):
    step = pl.program_id(0)
    blocks = out_ref.shape[1]
    rows = back_ref.shape[0]
    chunk = 256

    @pl.when(step == 0)
    def _():
        def widen(k, carry):
            at = pl.multiple_of(k * chunk, chunk)
            back_f[pl.ds(at, chunk), :] = back_ref[pl.ds(at, chunk), :].astype(F32)
            return carry

        lax.fori_loop(0, rows // chunk, widen, 0)

    for i in range(group):
        b = step * group + i
        total = jnp.zeros((C, PP), F32)
        for half in range(2):
            got = []
            for part_j in range(2):
                at = place_ref[b * K + 2 * half + part_j]
                values = back_f[pl.ds(jnp.maximum(at, 0), C, stride=slots), :]
                got.append(jnp.where(at >= 0, values, 0.0).astype(BF16))
            pair = jnp.concatenate([weight_ref[i, 2 * half], weight_ref[i, 2 * half + 1]], axis=1)
            total = total + lax.dot_general(
                jnp.concatenate(got, axis=1), pair, (((1,), (1,)), ((), ())), preferred_element_type=F32
            )
        out_f[pl.ds(b, C, stride=blocks), :] = total

    @pl.when(step == pl.num_programs(0) - 1)
    def _():
        for c in range(C):
            out_ref[c] = out_f[c * blocks : (c + 1) * blocks, :].astype(BF16)


def return_call(place, back, weights, slots):
    blocks = weights.shape[0]
    group = 8
    return pl.pallas_call(
        functools.partial(return_kernel, slots, group),
        grid=(blocks // group,),
        in_specs=[
            smem(),
            whole(back.shape),
            pl.BlockSpec((group, K, PP, PP), lambda g: (g, 0, 0, 0)),
        ],
        out_specs=whole((C, blocks, PP)),
        out_shape=jax.ShapeDtypeStruct((C, blocks, PP), BF16),
        scratch_shapes=[
            pltpu.VMEM((back.shape[0] + CP * slots, PP), F32),
            pltpu.VMEM((CP * blocks, PP), F32),
        ],
        compiler_params=params(),
        name="block_gradients",
    )(place, back, weights)


def shift(value, axis, by, wrap):
    count = lax.axis_size(axis)
    pairs = [(i, (i + by) % count) for i in range(count) if wrap or 0 <= i + by < count]
    return lax.ppermute(value, axis, pairs)


def local(latlon, intersection_weight, target_dev, target_piece, counts, conv_weight, cotangent):
    devices = lax.axis_size("face") * lax.axis_size("tile")
    blocks = latlon.shape[0]
    slots = max(2, (blocks * K + devices - 1) // devices)
    part = -(-C * slots // TILE) * TILE + TILE

    lat = jnp.swapaxes(latlon, 0, 1)
    send, place = send_call(target_dev, target_piece, counts, lat, intersection_weight, devices, slots, part)
    recv = lax.all_to_all(send.reshape(devices, part, PP), BOTH, split_axis=0, concat_axis=0, tiled=True)

    taps = jnp.pad(conv_weight.reshape(3, 3, HID, C), ((0, 0), (0, 0), (0, 0), (0, CP - C)))
    forward = taps.transpose(0, 2, 1, 3).reshape(3, HID, 3 * CP)
    backward = taps.transpose(0, 1, 3, 2).reshape(3, 3 * CP, HID)
    cot = jnp.swapaxes(cotangent[0], 0, 1)
    cot_top = shift(cotangent[0, :, ROWS - 1, :], "tile", 1, False)
    cot_bottom = shift(cotangent[0, :, 0, :], "tile", -1, False)

    def rim(at):
        inner = cotangent[0, :, :, at]
        return jnp.concatenate([cot_top[:, at : at + 1], inner, cot_bottom[:, at : at + 1]], axis=1)

    cot_west = shift(rim(COLS - 1), "face", 1, True)
    cot_east = shift(rim(0), "face", -1, True)
    gap = jnp.zeros((HID, 64 - ROWS - 2), BF16)
    cot_cols = jnp.concatenate([cot_west, gap, cot_east, gap], axis=1)

    field, low, high, west, east, pick = gather_call(recv, slots)
    top = shift(high, "tile", 1, False)
    bottom = shift(low, "tile", -1, False)
    west, east = columns_call(west, east, top, bottom)
    far_west = shift(east, "face", 1, True)
    far_east = shift(west, "face", -1, True)
    act, grad, reply = conv_call(
        slots, part, field, top, bottom, west, east, far_west, far_east, cot, cot_top, cot_bottom, cot_cols, forward, backward, pick
    )
    activation = jnp.swapaxes(act, 0, 1)[None]
    grad = lax.psum(lax.psum(grad, "tile"), "face")
    grad = grad * (1.0 / math.sqrt(devices * ROWS * COLS))
    grad_conv = jnp.swapaxes(grad.reshape(9, CP, HID)[:, :C, :], 1, 2)

    back = lax.all_to_all(reply, BOTH, split_axis=0, concat_axis=0, tiled=True)
    back = back.reshape(devices * (part - TILE), PP)
    grad_lat = return_call(place, back, intersection_weight, slots)
    return (activation, grad_conv, jnp.swapaxes(grad_lat, 0, 1))


def solution(mesh):
    placed = (
        P(BOTH, None, None),
        P(BOTH, None, None, None),
        P(BOTH, None),
        P(BOTH, None),
        P(BOTH),
        P(),
        P("face", None, "tile", None),
    )
    return jax.shard_map(
        local,
        mesh=mesh,
        in_specs=placed,
        out_specs=(P("face", None, "tile", None), P(), P(BOTH, None, None)),
        check_vma=False,
    )
```

```python
import functools
import math

import jax
import jax.numpy as jnp
from jax import lax
from jax.experimental import pallas as pl
from jax.experimental.pallas import tpu as pltpu
from jax.sharding import PartitionSpec as P

C = 74
CP = 80
HID = 256
ROWS = 16
COLS = 512
PP = 128
K = 4
PIECES = 64
TILE = 16
GRAD_ROWS = 768
BOTH = ("face", "tile")
VMEM_LIMIT = 58 * 1024 * 1024
F32 = jnp.float32
BF16 = jnp.bfloat16


def params():
    return pltpu.CompilerParams(vmem_limit_bytes=VMEM_LIMIT)


def whole(shape):
    return pl.BlockSpec(shape, lambda *_: (0,) * len(shape))


def smem():
    return pl.BlockSpec(memory_space=pltpu.SMEM)


def send_kernel(
    slots, part, dev_ref, piece_ref, counts_ref, lat_hbm, weight_hbm, send_ref, place_ref, lat, weights, lat_f, store, packed, tally, lat_sem, in_sem, out_sem
):
    blocks = lat.shape[1]
    devices = send_ref.shape[0] // part
    trash = devices * part
    codes = part - TILE
    chunks = in_sem.shape[0]
    group = blocks // chunks
    ships = out_sem.shape[0]
    share = devices // ships

    def load(k):
        rows = pl.ds(k * group, group)
        return pltpu.make_async_copy(weight_hbm.at[rows], weights.at[rows], in_sem.at[k])

    def ship(k):
        rows = pl.ds(k * share * part, share * part)
        return pltpu.make_async_copy(packed.at[rows], send_ref.at[rows], out_sem.at[k])

    fetch = pltpu.make_async_copy(lat_hbm, lat, lat_sem)
    fetch.start()
    for k in range(chunks):
        load(k).start()

    def clear(d, carry):
        tally[d] = 0
        at = pl.multiple_of(d * part, TILE)
        store[pl.ds(at, codes), :] = jnp.zeros((codes, PP), F32)
        store[pl.ds(at + codes, TILE), :] = jnp.full((TILE, PP), -1.0, F32)
        return carry

    lax.fori_loop(0, devices, clear, 0)

    def settle(b, carry):
        for j in range(K):
            live = j < counts_ref[b]
            d = dev_ref[j, b]
            s = tally[d]
            tally[d] = s + live.astype(jnp.int32)
            place_ref[b * K + j] = jnp.where(live, d * part + s, trash)
        return carry

    lax.fori_loop(0, blocks, settle, 0, unroll=4)
    fetch.wait()
    for c in range(C):
        lat_f[c * blocks : (c + 1) * blocks, :] = lat[c].astype(F32)

    def products(k, carry):
        load(k).wait()
        for i in range(group):
            b = k * group + i
            rows = lat_f[pl.ds(b, C, stride=blocks), :].astype(BF16)
            for half in range(2):
                pair = jnp.concatenate([weights[b, 2 * half], weights[b, 2 * half + 1]], axis=1)
                product = jnp.dot(rows, pair, preferred_element_type=F32)
                for part_j in range(2):
                    j = 2 * half + part_j
                    at = place_ref[b * K + j]
                    store[pl.ds(at, C, stride=slots), :] = product[:, part_j * PP : (part_j + 1) * PP]
                    code = jnp.full((TILE // slots, PP), piece_ref[j, b].astype(F32), F32)
                    store[pl.ds(at + codes, TILE // slots, stride=slots), :] = code
        return carry

    lax.fori_loop(0, chunks, products, 0)
    for k in range(ships):

        def pack(d, carry):
            at = pl.multiple_of((k * share + d) * part, TILE)
            packed[pl.ds(at, part), :] = store[pl.ds(at, part), :].astype(BF16)
            return carry

        lax.fori_loop(0, share, pack, 0)
        ship(k).start()
    for k in range(ships):
        ship(k).wait()


def anywhere():
    return pl.BlockSpec(memory_space=pl.ANY)


def send_call(dev, piece, counts, lat, weights, devices, slots, part):
    blocks = lat.shape[1]
    return pl.pallas_call(
        functools.partial(send_kernel, slots, part),
        in_specs=[smem(), smem(), smem(), anywhere(), anywhere()],
        out_specs=[anywhere(), smem()],
        out_shape=[
            jax.ShapeDtypeStruct((devices * part, PP), BF16),
            jax.ShapeDtypeStruct((blocks * K,), jnp.int32),
        ],
        scratch_shapes=[
            pltpu.VMEM(lat.shape, BF16),
            pltpu.VMEM(weights.shape, BF16),
            pltpu.VMEM((CP * blocks, PP), F32),
            pltpu.VMEM((devices * part + part + CP * slots, PP), F32),
            pltpu.VMEM((devices * part, PP), BF16),
            pltpu.SMEM((devices,), jnp.int32),
            pltpu.SemaphoreType.DMA,
            pltpu.SemaphoreType.DMA((4,)),
            pltpu.SemaphoreType.DMA((8,)),
        ],
        compiler_params=params(),
        name="block_products",
    )(dev, piece, counts, lat, weights)


def lane_of(shape):
    return lax.broadcasted_iota(jnp.int32, shape, 1)


def put_columns(message, row, lane, first, second):
    message = jnp.where(lane == row, first, message)
    return jnp.where(lane == 32 + row, second, message)


def gather_kernel(slots, recv_hbm, field_ref, low_ref, high_ref, west_ref, east_ref, pick_ref, recv_ref, total, sem):
    devices, part = recv_ref.shape[0], recv_ref.shape[1]
    per = TILE // slots
    tiles = part // TILE - 1
    keys = devices * TILE
    step = -(-tiles // 8) * 2
    cuts = list(range(0, tiles, step)) + [tiles]

    def load(k):
        first, end = (tiles, tiles + 1) if k == 0 else (cuts[k - 1], cuts[k])
        rows = pl.ds(first * TILE, (end - first) * TILE)
        return pltpu.make_async_copy(recv_hbm.at[:, rows, :], recv_ref.at[:, rows, :], sem.at[k])

    for k in range(len(cuts)):
        load(k).start()
    load(0).wait()
    codes = recv_ref[:, part - TILE :, :].astype(F32).reshape(keys, PP).astype(jnp.int32)
    within = lax.rem(lax.broadcasted_iota(jnp.int32, (keys, PP), 0), TILE)
    codes = jnp.where(codes < 0, -4096, codes + within // slots * PIECES)
    wide = per * PIECES
    picks = []
    for t in range(wide // PP):
        picks.append((codes == lane_of((keys, PP)) + t * PP).astype(F32))
    pick = jnp.concatenate(picks, axis=1) if len(picks) > 1 else picks[0]
    pick_ref[...] = pick.astype(BF16)
    pick_t = jnp.transpose(pick).astype(BF16)
    total[...] = jnp.zeros(total.shape, F32)
    for t in range(0, tiles, 2):
        if t in cuts:
            load(cuts.index(t) + 1).wait()
        pair = [t, t + 1] if t + 1 < tiles else [t]
        data = [recv_ref[:, u * TILE : (u + 1) * TILE, :].reshape(keys, PP) for u in pair]
        data = jnp.concatenate(data, axis=1) if len(data) > 1 else data[0]
        sums = jnp.dot(pick_t, data, preferred_element_type=F32)
        for n, u in enumerate(pair):
            for p in range(per):
                c = u * per + p
                if c < C:
                    total[pl.ds(c, PIECES, stride=CP), :] = sums[
                        p * PIECES : (p + 1) * PIECES, n * PP : (n + 1) * PP
                    ]
    lane = lane_of((CP, PP))
    west = jnp.zeros((CP, PP), F32)
    east = jnp.zeros((CP, PP), F32)
    quarters = COLS // PP
    for r in range(ROWS):
        for q in range(quarters):
            piece = r * quarters + q
            block = total[piece * CP : (piece + 1) * CP, :]
            out = block.astype(BF16)
            field_ref[r, :, q * PP : (q + 1) * PP] = out
            if r < 2:
                low_ref[r, :, q * PP : (q + 1) * PP] = out
            if r >= ROWS - 2:
                high_ref[r - ROWS + 2, :, q * PP : (q + 1) * PP] = out
            if q == 0:
                west = put_columns(west, r + 2, lane, block[:, 0:1], block[:, 1:2])
            if q == quarters - 1:
                east = put_columns(east, r + 2, lane, block[:, PP - 2 : PP - 1], block[:, PP - 1 : PP])
    west_ref[...] = west.astype(BF16)
    east_ref[...] = east.astype(BF16)


def gather_call(recv, slots):
    devices = recv.shape[0]
    wide = TILE // slots * PIECES
    shapes = [(ROWS, CP, COLS), (2, CP, COLS), (2, CP, COLS), (CP, PP), (CP, PP), (devices * TILE, wide)]
    return pl.pallas_call(
        functools.partial(gather_kernel, slots),
        grid=(1,),
        in_specs=[anywhere()],
        out_specs=[whole(s) for s in shapes],
        out_shape=[jax.ShapeDtypeStruct(s, BF16) for s in shapes],
        scratch_shapes=[
            pltpu.VMEM(recv.shape, BF16),
            pltpu.VMEM((PIECES * CP, PP), F32),
            pltpu.SemaphoreType.DMA((8,)),
        ],
        compiler_params=params(),
        name="field_sum",
    )(recv)


def columns_kernel(west0, east0, top_ref, bottom_ref, west_ref, east_ref):
    lane = lane_of((CP, PP))
    west = west0[...].astype(F32)
    east = east0[...].astype(F32)
    for row, ref, i in ((0, top_ref, 0), (1, top_ref, 1), (ROWS + 2, bottom_ref, 0), (ROWS + 3, bottom_ref, 1)):
        left = ref[i, :, 0:PP].astype(F32)
        right = ref[i, :, COLS - PP : COLS].astype(F32)
        west = put_columns(west, row, lane, left[:, 0:1], left[:, 1:2])
        east = put_columns(east, row, lane, right[:, PP - 2 : PP - 1], right[:, PP - 1 : PP])
    west_ref[...] = west.astype(BF16)
    east_ref[...] = east.astype(BF16)


def columns_call(west, east, top, bottom):
    return pl.pallas_call(
        columns_kernel,
        out_shape=[jax.ShapeDtypeStruct((CP, PP), BF16)] * 2,
        name="edge_columns",
    )(west, east, top, bottom)


def gelu_parts(value):
    square = value * value
    tanh_part = jnp.tanh(value * (0.7978845608 + (0.7978845608 * 0.044715) * square))
    half = 0.5 + 0.5 * tanh_part
    inner = (0.5 * 0.7978845608) + (0.5 * 0.7978845608 * 0.134145) * square
    slope = half + value * inner * (1.0 - tanh_part * tanh_part)
    return (value * half, slope)


def conv_kernel(
    slots,
    field_ref,
    top_ref,
    bottom_ref,
    own_west,
    own_east,
    far_west,
    far_east,
    cot_hbm,
    cot_top,
    cot_bottom,
    cot_cols,
    forward_ref,
    backward_ref,
    pick_ref,
    act_hbm,
    grad_ref,
    reply_ref,
    stack,
    dpre,
    cots,
    acts,
    side,
    dfield,
    packed,
    in_sem,
    out_sem,
    sem,
):
    step = pl.program_id(0)
    lane = lane_of((CP, PP))
    lane_wide = lane_of((CP, COLS))
    taps = 9 * CP

    def column(ref, at):
        return jnp.sum(jnp.where(lane == at, ref[...].astype(F32), 0.0), axis=1, keepdims=True)

    def build(row, rows):
        before = column(far_west, 32 + row)
        after = column(far_east, row)
        middle = rows.astype(F32)
        left = jnp.where(lane_wide == 0, before, pltpu.roll(middle, 1, 1))
        right = jnp.where(lane_wide == COLS - 1, after, pltpu.roll(middle, COLS - 1, 1))
        stack[row, 0:CP, :] = left.astype(BF16)
        stack[row, CP : 2 * CP, :] = rows
        stack[row, 2 * CP : 3 * CP, :] = right.astype(BF16)

    def load(k):
        if k < 4:
            return pltpu.make_async_copy(cot_hbm.at[pl.ds(4 * k, 4)], cots.at[pl.ds(4 * k + 1, 4)], in_sem.at[k])
        ref, row = (cot_top, 0) if k == 4 else (cot_bottom, ROWS + 1)
        return pltpu.make_async_copy(ref, cots.at[row], in_sem.at[k])

    def ship_act(k):
        return pltpu.make_async_copy(acts.at[pl.ds(4 * k + 1, 4)], act_hbm.at[pl.ds(4 * k, 4)], out_sem.at[k])

    @pl.when(step == 0)
    def _():
        for k in (4, 0, 1, 2, 3, 5):
            load(k).start()
        build(0, top_ref[0])
        build(1, top_ref[1])
        build(2, field_ref[0])
        build(3, field_ref[1])
        grad_ref[...] = jnp.zeros(grad_ref.shape, F32)
        wests = [far_west[...].astype(F32)] * 2 + [own_west[...].astype(F32)]
        easts = [own_east[...].astype(F32)] + [far_east[...].astype(F32)] * 2
        west_at = (0, 32, 0)
        east_at = (32, 0, 32)
        parts = []
        for ky in range(3):
            for kx in range(3):
                w = pltpu.roll(wests[kx], (2 * PP - west_at[kx] - ky) % PP, 1)
                e = pltpu.roll(easts[kx], (2 * PP + 64 - east_at[kx] - ky) % PP, 1)
                parts.append(jnp.where(lane < 64, w, e))
        columns = jnp.concatenate(parts, axis=0).astype(BF16)
        pre = jnp.dot(forward_ref[...], columns, preferred_element_type=F32)
        unused, slope = gelu_parts(pre)
        dcol = (cot_cols[...].astype(F32) * slope).astype(BF16).astype(F32)
        moved = [dcol] + [pltpu.roll(dcol, PP - m, 1) for m in (1, 2)]
        side[...] = jnp.dot(
            backward_ref[...], jnp.concatenate(moved, axis=0).astype(BF16), preferred_element_type=F32
        )
        load(4).wait()
        load(0).wait()

    for k in (1, 2, 3):

        @pl.when(step == 2 * k)
        def _():
            load(k).wait()

    @pl.when(step == ROWS // 2)
    def _():
        load(5).wait()

    @pl.when(step <= ROWS // 2)
    def _():
        for i in range(2):
            p = 2 * step + i
            pre = jnp.dot(
                forward_ref[...], stack[pl.ds(p, 3)].reshape(taps, COLS), preferred_element_type=F32
            )
            result, slope = gelu_parts(pre)
            dpre[p] = (cots[p].astype(F32) * slope).astype(BF16)
            acts[p] = result.astype(BF16)

    for k in range(4):

        @pl.when(step == 2 * k + 2)
        def _():
            ship_act(k).start()

    @pl.when(step < ROWS // 2 - 1)
    def _():
        for i in range(2):
            build(2 * step + 4 + i, field_ref[2 * step + 2 + i])

    @pl.when(step == ROWS // 2 - 1)
    def _():
        for i in range(2):
            build(ROWS + 2 + i, bottom_ref[i])

    @pl.when(step >= 2)
    def _():
        quarters = COLS // PP
        for i in range(2):
            r = 2 * (step - 2) + i
            out = jnp.dot(
                backward_ref[...], dpre[pl.ds(r, 3)].reshape(3 * HID, COLS), preferred_element_type=F32
            )
            after = jnp.sum(jnp.where(lane == 64 + r, side[0:CP, :], 0.0), axis=1, keepdims=True)
            before = jnp.sum(jnp.where(lane == r, side[2 * CP :, :], 0.0), axis=1, keepdims=True)
            rows = (
                jnp.where(lane_wide == COLS - 1, after, pltpu.roll(out[0:CP], COLS - 1, 1))
                + out[CP : 2 * CP]
                + jnp.where(lane_wide == 0, before, pltpu.roll(out[2 * CP :], 1, 1))
            )
            for q in range(quarters):
                at = pl.multiple_of((r * quarters + q) * CP, 8)
                dfield[pl.ds(at, CP), :] = rows[:, q * PP : (q + 1) * PP]
        first = 2 * (step - 2) + 1
        fields = [stack[pl.ds(first + i, 3)].reshape(taps, COLS) for i in range(2)]
        owns = [dpre[first + i] for i in range(2)]
        grad_ref[0:taps, :] += lax.dot_general(
            jnp.concatenate(fields, axis=1),
            jnp.concatenate(owns, axis=1),
            (((1,), (1,)), ((), ())),
            preferred_element_type=F32,
        )

    @pl.when(step == ROWS // 2 + 1)
    def _():
        devices = packed.shape[0]
        per = TILE // slots
        tiles = packed.shape[1] // TILE
        ships = sem.shape[0]
        cut = -(-tiles // (2 * ships)) * 2
        pick = pick_ref[...]

        def ship(k):
            rows = pl.ds(k * cut * TILE, (min(tiles, (k + 1) * cut) - k * cut) * TILE)
            return pltpu.make_async_copy(packed.at[:, rows, :], reply_ref.at[:, rows, :], sem.at[k])

        started = []
        for t in range(0, tiles, 2):
            pair = [t, t + 1] if t + 1 < tiles else [t]
            data = []
            for u in pair:
                chans = [
                    dfield[pl.ds(min(u * per + p, CP - 1), PIECES, stride=CP), :].astype(BF16) for p in range(per)
                ]
                data.append(jnp.concatenate(chans, axis=0) if per > 1 else chans[0])
            data = jnp.concatenate(data, axis=1) if len(data) > 1 else data[0]
            got = jnp.dot(pick, data, preferred_element_type=F32).astype(BF16)
            for n, u in enumerate(pair):
                packed[:, u * TILE : (u + 1) * TILE, :] = got[:, n * PP : (n + 1) * PP].reshape(devices, TILE, PP)
            if (t + 2) % cut == 0 or t + 2 >= tiles:
                k = t // cut
                ship(k).start()
                started.append(k)
        for k in range(4):
            ship_act(k).wait()
        for k in started:
            ship(k).wait()


def conv_call(slots, part, field, top, bottom, own_west, own_east, far_west, far_east, cot, cot_top, cot_bottom, cot_cols, forward, backward, pick):
    devices = pick.shape[0] // TILE
    reply_rows = part - TILE
    edges = [whole(x.shape) for x in (field, top, bottom, own_west, own_east, far_west, far_east)]
    return pl.pallas_call(
        functools.partial(conv_kernel, slots),
        grid=(ROWS // 2 + 2,),
        in_specs=edges
        + [anywhere(), anywhere(), anywhere()]
        + [whole(x.shape) for x in (cot_cols, forward, backward, pick)],
        out_specs=[anywhere(), whole((GRAD_ROWS, HID)), anywhere()],
        out_shape=[
            jax.ShapeDtypeStruct((ROWS, HID, COLS), BF16),
            jax.ShapeDtypeStruct((GRAD_ROWS, HID), F32),
            jax.ShapeDtypeStruct((devices, reply_rows, PP), BF16),
        ],
        scratch_shapes=[
            pltpu.VMEM((ROWS + 4, 3 * CP, COLS), BF16),
            pltpu.VMEM((ROWS + 2, HID, COLS), BF16),
            pltpu.VMEM((ROWS + 2, HID, COLS), BF16),
            pltpu.VMEM((ROWS + 2, HID, COLS), BF16),
            pltpu.VMEM((3 * CP, PP), F32),
            pltpu.VMEM((PIECES * CP, PP), F32),
            pltpu.VMEM((devices, reply_rows, PP), BF16),
            pltpu.SemaphoreType.DMA((6,)),
            pltpu.SemaphoreType.DMA((4,)),
            pltpu.SemaphoreType.DMA((4,)),
        ],
        compiler_params=params(),
        name="conv_level",
    )(field, top, bottom, own_west, own_east, far_west, far_east, cot, cot_top, cot_bottom, cot_cols, forward, backward, pick)


def return_kernel(slots, devices, place_ref, back_hbm, weight_hbm, out_ref, back, weights, back_f, out_f, back_sem, in_sem):
    blocks = out_ref.shape[1]
    chunks = in_sem.shape[0]
    group = blocks // chunks
    cuts = back_sem.shape[0]
    size = back.shape[0] // cuts
    share = devices // cuts
    rows = back.shape[0] // devices
    part = rows + TILE
    trash = devices * part

    def fetch(k):
        span = pl.ds(k * size, size)
        return pltpu.make_async_copy(back_hbm.at[span], back.at[span], back_sem.at[k])

    def load(k):
        rows = pl.ds(k * group, group)
        return pltpu.make_async_copy(weight_hbm.at[rows], weights.at[rows], in_sem.at[k])

    for k in range(cuts):
        fetch(k).start()
    for k in range(chunks):
        load(k).start()

    def widen(k, carry):
        fetch(k).wait()
        for i in range(share):
            at = pl.multiple_of((k * share + i) * rows, TILE)
            to = pl.multiple_of((k * share + i) * part, TILE)
            back_f[pl.ds(to, rows), :] = back[pl.ds(at, rows), :].astype(F32)
        return carry

    lax.fori_loop(0, cuts, widen, 0)
    back_f[pl.ds(trash, CP * slots), :] = jnp.zeros((CP * slots, PP), F32)

    def gradients(k, carry):
        load(k).wait()
        for i in range(group):
            b = k * group + i
            total = jnp.zeros((C, PP), F32)
            for half in range(2):
                got = []
                for part_j in range(2):
                    at = place_ref[b * K + 2 * half + part_j]
                    got.append(back_f[pl.ds(at, C, stride=slots), :].astype(BF16))
                pair = jnp.concatenate([weights[b, 2 * half], weights[b, 2 * half + 1]], axis=1)
                total = total + lax.dot_general(
                    jnp.concatenate(got, axis=1), pair, (((1,), (1,)), ((), ())), preferred_element_type=F32
                )
            out_f[pl.ds(b, C, stride=blocks), :] = total
        return carry

    lax.fori_loop(0, chunks, gradients, 0)
    for c in range(C):
        out_ref[c] = out_f[c * blocks : (c + 1) * blocks, :].astype(BF16)


def return_call(place, back, weights, devices, slots):
    blocks = weights.shape[0]
    return pl.pallas_call(
        functools.partial(return_kernel, slots, devices),
        grid=(1,),
        in_specs=[smem(), anywhere(), anywhere()],
        out_specs=whole((C, blocks, PP)),
        out_shape=jax.ShapeDtypeStruct((C, blocks, PP), BF16),
        scratch_shapes=[
            pltpu.VMEM(back.shape, BF16),
            pltpu.VMEM(weights.shape, BF16),
            pltpu.VMEM((back.shape[0] + devices * TILE + CP * slots, PP), F32),
            pltpu.VMEM((CP * blocks, PP), F32),
            pltpu.SemaphoreType.DMA((8,)),
            pltpu.SemaphoreType.DMA((2,)),
        ],
        compiler_params=params(),
        name="block_gradients",
    )(place, back, weights)


def shift(value, face_by, tile_by):
    faces, tiles = lax.axis_size("face"), lax.axis_size("tile")
    pairs = [
        (f * tiles + t, (f + face_by) % faces * tiles + t + tile_by)
        for f in range(faces)
        for t in range(tiles)
        if 0 <= t + tile_by < tiles
    ]
    return lax.ppermute(value, BOTH, pairs)


def swap(value, axis, bit):
    return lax.ppermute(value, axis, [(i, i ^ (1 << bit)) for i in range(lax.axis_size(axis))])


def upper(axis, bit):
    return (lax.axis_index(axis) >> bit) & 1


def fold(value, axis, bit):
    half = value.shape[0] // 2
    mine = upper(axis, bit)
    keep = lax.dynamic_slice_in_dim(value, mine * half, half, axis=0)
    send = lax.dynamic_slice_in_dim(value, (1 - mine) * half, half, axis=0)
    return keep + swap(send, axis, bit)


def unfold(value, axis, bit):
    got = swap(value, axis, bit)
    first = upper(axis, bit) == 0
    return jnp.concatenate([jnp.where(first, value, got), jnp.where(first, got, value)], axis=0)


def local(latlon, intersection_weight, target_dev, target_piece, counts, conv_weight, cotangent):
    faces, tiles = lax.axis_size("face"), lax.axis_size("tile")
    devices = faces * tiles
    blocks = latlon.shape[0]
    slots = max(2, (blocks * K + devices - 1) // devices)
    part = -(-C * slots // TILE) * TILE + TILE

    lat = jnp.swapaxes(latlon, 0, 1)
    send, place = send_call(
        target_dev.T, target_piece.T, counts, lat, intersection_weight, devices, slots, part
    )
    recv = lax.all_to_all(send.reshape(devices, part, PP), BOTH, split_axis=0, concat_axis=0, tiled=True)

    taps = jnp.pad(conv_weight.reshape(3, 3, HID, C), ((0, 0), (0, 0), (0, 0), (0, CP - C)))
    forward = taps.transpose(2, 0, 1, 3).reshape(HID, 9 * CP)
    backward = taps[::-1].transpose(1, 3, 0, 2).reshape(3 * CP, 3 * HID)
    cot = jnp.swapaxes(cotangent[0], 0, 1)
    cot_top = shift(cotangent[0, :, ROWS - 1, :], 0, 1)
    cot_bottom = shift(cotangent[0, :, 0, :], 0, -1)

    def rim(at, face_by):
        column = cotangent[0, :, :, at]
        above = shift(column[:, ROWS - 1 :], face_by, 1)
        below = shift(column[:, :1], face_by, -1)
        return [above, shift(column, face_by, 0), below]

    gap = [jnp.zeros((HID, 64 - ROWS - 2), BF16)]
    cot_cols = jnp.concatenate(rim(COLS - 1, 1) + gap + rim(0, -1) + gap, axis=1)
    recv, forward, backward, cot, cot_top, cot_bottom, cot_cols = lax.optimization_barrier(
        (recv, forward, backward, cot, cot_top, cot_bottom, cot_cols)
    )

    field, low, high, west, east, pick = gather_call(recv, slots)
    top = shift(high, 0, 1)
    bottom = shift(low, 0, -1)
    west, east = columns_call(west, east, top, bottom)
    far_west = shift(east, 1, 0)
    far_east = shift(west, -1, 0)
    act, grad, reply = conv_call(
        slots, part, field, top, bottom, west, east, far_west, far_east, cot, cot_top, cot_bottom, cot_cols, forward, backward, pick
    )
    activation = jnp.swapaxes(act, 0, 1)[None]

    back = lax.all_to_all(reply, BOTH, split_axis=0, concat_axis=0, tiled=True)

    halves = [("tile", 0)] + [("face", bit) for bit in range((faces - 1).bit_length())]
    for axis, bit in halves:
        grad = fold(grad, axis, bit)
    groups = [list(range(first, tiles, 2)) for first in range(2)]
    grad = lax.psum(grad, "tile", axis_index_groups=groups)
    grad = grad * (1.0 / math.sqrt(devices * ROWS * COLS))
    for axis, bit in reversed(halves):
        grad = unfold(grad, axis, bit)
    grad_conv = jnp.swapaxes(grad[: 9 * CP].reshape(9, CP, HID)[:, :C, :], 1, 2)

    back = back.reshape(devices * (part - TILE), PP)
    grad_lat = return_call(place, back, intersection_weight, devices, slots)
    return (activation, grad_conv, jnp.swapaxes(grad_lat, 0, 1))


def solution(mesh):
    placed = (
        P(BOTH, None, None),
        P(BOTH, None, None, None),
        P(BOTH, None),
        P(BOTH, None),
        P(BOTH),
        P(),
        P("face", None, "tile", None),
    )
    return jax.shard_map(
        local,
        mesh=mesh,
        in_specs=placed,
        out_specs=(P("face", None, "tile", None), P(), P(BOTH, None, None)),
        check_vma=False,
    )
```

```python
import functools
import math

import jax
import jax.numpy as jnp
from jax import lax
from jax.experimental import pallas as pl
from jax.experimental.layout import Layout, with_layout_constraint
from jax.experimental.pallas import tpu as pltpu
from jax.sharding import PartitionSpec as P

C = 74
CP = 80
HID = 256
ROWS = 16
COLS = 512
PP = 128
K = 4
PIECES = 64
TILE = 16
GRAD_ROWS = 768
BOTH = ("face", "tile")
VMEM_LIMIT = 58 * 1024 * 1024
F32 = jnp.float32
BF16 = jnp.bfloat16


def params():
    return pltpu.CompilerParams(vmem_limit_bytes=VMEM_LIMIT)


def whole(shape):
    return pl.BlockSpec(shape, lambda *_: (0,) * len(shape))


def smem():
    return pl.BlockSpec(memory_space=pltpu.SMEM)


def send_kernel(
    slots, part, dev_ref, piece_ref, counts_ref, lat_hbm, weight_hbm, send_ref, place_ref, lat, weights, lat_f, store, packed, tally, lat_sem, in_sem, out_sem
):
    blocks = lat.shape[1]
    devices = send_ref.shape[0] // part
    trash = devices * part
    codes = part - TILE
    chunks = in_sem.shape[0]
    group = blocks // chunks
    ships = out_sem.shape[0]
    share = devices // ships

    def slot_of(rows):
        return lax.rem(lax.broadcasted_iota(jnp.int32, (rows, PP), 0), slots)

    def load(k):
        rows = pl.ds(k * group, group)
        return pltpu.make_async_copy(weight_hbm.at[rows], weights.at[rows], in_sem.at[k])

    def ship(k):
        rows = pl.ds(k * share * part, share * part)
        return pltpu.make_async_copy(packed.at[rows], send_ref.at[rows], out_sem.at[k])

    fetch = pltpu.make_async_copy(lat_hbm, lat, lat_sem)
    fetch.start()
    for k in range(chunks):
        load(k).start()

    def clear(d, carry):
        tally[d] = 0
        return carry

    lax.fori_loop(0, devices, clear, 0)

    def settle(b, carry):
        for j in range(K):
            live = j < counts_ref[b]
            d = dev_ref[j, b]
            s = tally[d]
            tally[d] = s + live.astype(jnp.int32)
            place_ref[b * K + j] = jnp.where(live, d * part + s, trash)
        return carry

    lax.fori_loop(0, blocks, settle, 0, unroll=4)
    fetch.wait()
    for c in range(C):
        lat_f[c * blocks : (c + 1) * blocks, :] = lat[c].astype(F32)

    def products(k, carry):
        load(k).wait()
        for i in range(group):
            b = k * group + i
            rows = lat_f[pl.ds(b, C, stride=blocks), :].astype(BF16)
            for half in range(2):
                pair = jnp.concatenate([weights[b, 2 * half], weights[b, 2 * half + 1]], axis=1)
                product = jnp.dot(rows, pair, preferred_element_type=F32)
                for part_j in range(2):
                    j = 2 * half + part_j
                    at = place_ref[b * K + j]
                    store[pl.ds(at, C, stride=slots), :] = product[:, part_j * PP : (part_j + 1) * PP]
                    code = jnp.full((TILE // slots, PP), piece_ref[j, b].astype(F32), F32)
                    store[pl.ds(at + codes, TILE // slots, stride=slots), :] = code
        return carry

    lax.fori_loop(0, chunks, products, 0)
    for k in range(ships):

        def pack(d, carry):
            used = tally[k * share + d]
            at = pl.multiple_of((k * share + d) * part, TILE)
            values = jnp.where(slot_of(codes) < used, store[pl.ds(at, codes), :], 0.0)
            packed[pl.ds(at, codes), :] = values.astype(BF16)
            subtiles = jnp.where(slot_of(TILE) < used, store[pl.ds(at + codes, TILE), :], -1.0)
            packed[pl.ds(at + codes, TILE), :] = subtiles.astype(BF16)
            return carry

        lax.fori_loop(0, share, pack, 0)
        ship(k).start()
    for k in range(ships):
        ship(k).wait()


def anywhere():
    return pl.BlockSpec(memory_space=pl.ANY)


def send_call(dev, piece, counts, lat, weights, devices, slots, part):
    blocks = lat.shape[1]
    return pl.pallas_call(
        functools.partial(send_kernel, slots, part),
        in_specs=[smem(), smem(), smem(), anywhere(), anywhere()],
        out_specs=[anywhere(), smem()],
        out_shape=[
            jax.ShapeDtypeStruct((devices * part, PP), BF16),
            jax.ShapeDtypeStruct((blocks * K,), jnp.int32),
        ],
        scratch_shapes=[
            pltpu.VMEM(lat.shape, BF16),
            pltpu.VMEM(weights.shape, BF16),
            pltpu.VMEM((CP * blocks, PP), F32),
            pltpu.VMEM((devices * part + part + CP * slots, PP), F32),
            pltpu.VMEM((devices * part, PP), BF16),
            pltpu.SMEM((devices,), jnp.int32),
            pltpu.SemaphoreType.DMA,
            pltpu.SemaphoreType.DMA((4,)),
            pltpu.SemaphoreType.DMA((8,)),
        ],
        compiler_params=params(),
        name="block_products",
    )(dev, piece, counts, lat, weights)


def lane_of(shape):
    return lax.broadcasted_iota(jnp.int32, shape, 1)


def put_columns(message, row, lane, first, second):
    message = jnp.where(lane == row, first, message)
    return jnp.where(lane == 32 + row, second, message)


def taps_kernel(weight_ref, forward_ref, backward_ref, taps):
    taps[...] = jnp.zeros(taps.shape, F32)
    for k in range(9):
        taps[k * CP : k * CP + C, :] = weight_ref[k].astype(F32)
    forward_ref[...] = jnp.transpose(taps[...]).astype(BF16)[:, 0 : 9 * CP]
    for m in range(3):
        rows = slice((2 - m) * 3 * CP, (3 - m) * 3 * CP)
        backward_ref[:, m * HID : (m + 1) * HID] = taps[rows, :].astype(BF16)


def taps_call(weight):
    return pl.pallas_call(
        taps_kernel,
        out_shape=[
            jax.ShapeDtypeStruct((HID, 9 * CP), BF16),
            jax.ShapeDtypeStruct((3 * CP, 3 * HID), BF16),
        ],
        scratch_shapes=[pltpu.VMEM((GRAD_ROWS, HID), F32)],
        name="taps",
    )(weight)


def gather_kernel(slots, recv_hbm, first_ref, last_ref, field_ref, low_ref, high_ref, west_ref, east_ref, pick_ref, recv_ref, total, sem):
    devices, part = recv_ref.shape[0], recv_ref.shape[1]
    per = TILE // slots
    tiles = part // TILE - 1
    keys = devices * TILE
    step = -(-tiles // 8) * 2
    cuts = list(range(0, tiles, step)) + [tiles]

    def load(k):
        first, end = (tiles, tiles + 1) if k == 0 else (cuts[k - 1], cuts[k])
        rows = pl.ds(first * TILE, (end - first) * TILE)
        return pltpu.make_async_copy(recv_hbm.at[:, rows, :], recv_ref.at[:, rows, :], sem.at[k])

    for k in range(len(cuts)):
        load(k).start()
    load(0).wait()
    codes = recv_ref[:, part - TILE :, :].astype(F32).reshape(keys, PP).astype(jnp.int32)
    within = lax.rem(lax.broadcasted_iota(jnp.int32, (keys, PP), 0), TILE)
    codes = jnp.where(codes < 0, -4096, codes + within // slots * PIECES)
    wide = per * PIECES
    picks = []
    for t in range(wide // PP):
        picks.append((codes == lane_of((keys, PP)) + t * PP).astype(F32))
    pick = jnp.concatenate(picks, axis=1) if len(picks) > 1 else picks[0]
    pick_ref[...] = pick.astype(BF16)
    pick_t = jnp.transpose(pick).astype(BF16)
    total[...] = jnp.zeros(total.shape, F32)
    for t in range(0, tiles, 2):
        if t in cuts:
            load(cuts.index(t) + 1).wait()
        pair = [t, t + 1] if t + 1 < tiles else [t]
        data = [recv_ref[:, u * TILE : (u + 1) * TILE, :].reshape(keys, PP) for u in pair]
        data = jnp.concatenate(data, axis=1) if len(data) > 1 else data[0]
        sums = jnp.dot(pick_t, data, preferred_element_type=F32)
        for n, u in enumerate(pair):
            for p in range(per):
                c = u * per + p
                if c < C:
                    total[pl.ds(c, PIECES, stride=CP), :] = sums[
                        p * PIECES : (p + 1) * PIECES, n * PP : (n + 1) * PP
                    ]
    lane = lane_of((CP, PP))
    west = jnp.zeros((CP, PP), F32)
    east = jnp.zeros((CP, PP), F32)
    quarters = COLS // PP
    for r in range(ROWS):
        for q in range(quarters):
            piece = r * quarters + q
            block = total[piece * CP : (piece + 1) * CP, :]
            out = block.astype(BF16)
            field_ref[r, :, q * PP : (q + 1) * PP] = out
            if r < 2:
                low_ref[r * CP : (r + 1) * CP, q * PP : (q + 1) * PP] = out
            if r >= ROWS - 2:
                high_ref[(r - ROWS + 2) * CP : (r - ROWS + 3) * CP, q * PP : (q + 1) * PP] = out
            if q == 0:
                west = put_columns(west, r + 2, lane, block[:, 0:1], block[:, 1:2])
            if q == quarters - 1:
                east = put_columns(east, r + 2, lane, block[:, PP - 2 : PP - 1], block[:, PP - 1 : PP])
    west_ref[...] = west.astype(BF16)
    east_ref[...] = east.astype(BF16)
    low_ref[2 * CP :, :] = first_ref[...]
    high_ref[2 * CP :, :] = last_ref[...]


def gather_call(recv, first, last, slots):
    devices = recv.shape[0]
    wide = TILE // slots * PIECES
    edge = (2 * CP + HID, COLS)
    shapes = [(ROWS, CP, COLS), edge, edge, (CP, PP), (CP, PP), (devices * TILE, wide)]
    return pl.pallas_call(
        functools.partial(gather_kernel, slots),
        grid=(1,),
        in_specs=[anywhere(), whole(first.shape), whole(last.shape)],
        out_specs=[whole(s) for s in shapes],
        out_shape=[jax.ShapeDtypeStruct(s, BF16) for s in shapes],
        scratch_shapes=[
            pltpu.VMEM(recv.shape, BF16),
            pltpu.VMEM((PIECES * CP, PP), F32),
            pltpu.SemaphoreType.DMA((8,)),
        ],
        compiler_params=params(),
        name="field_sum",
    )(recv, first, last)


def columns_kernel(west0, east0, cot_west, cot_east, top_ref, bottom_ref, west_ref, east_ref):
    lane = lane_of((CP, PP))
    west = west0[...].astype(F32)
    east = east0[...].astype(F32)
    for row, ref, i in ((0, top_ref, 0), (1, top_ref, 1), (ROWS + 2, bottom_ref, 0), (ROWS + 3, bottom_ref, 1)):
        left = ref[i * CP : (i + 1) * CP, 0:PP].astype(F32)
        right = ref[i * CP : (i + 1) * CP, COLS - PP : COLS].astype(F32)
        west = put_columns(west, row, lane, left[:, 0:1], left[:, 1:2])
        east = put_columns(east, row, lane, right[:, PP - 2 : PP - 1], right[:, PP - 1 : PP])
    west_ref[0:CP, :] = west.astype(BF16)
    east_ref[0:CP, :] = east.astype(BF16)
    lane = lane_of((HID, PP))
    west = cot_west[...].astype(F32)
    east = cot_east[...].astype(F32)
    for row, ref in ((0, top_ref), (ROWS + 1, bottom_ref)):
        west = jnp.where(lane == row, ref[2 * CP :, 0:PP].astype(F32)[:, 0:1], west)
        east = jnp.where(lane == row, ref[2 * CP :, COLS - PP : COLS].astype(F32)[:, PP - 1 : PP], east)
    west_ref[CP:, :] = west.astype(BF16)
    east_ref[CP:, :] = east.astype(BF16)


def columns_call(west, east, cot_west, cot_east, top, bottom):
    return pl.pallas_call(
        columns_kernel,
        out_shape=[jax.ShapeDtypeStruct((CP + HID, PP), BF16)] * 2,
        name="edge_columns",
    )(west, east, cot_west, cot_east, top, bottom)


def gelu_parts(value):
    square = value * value
    tanh_part = jnp.tanh(value * (0.7978845608 + (0.7978845608 * 0.044715) * square))
    half = 0.5 + 0.5 * tanh_part
    inner = (0.5 * 0.7978845608) + (0.5 * 0.7978845608 * 0.134145) * square
    slope = half + value * inner * (1.0 - tanh_part * tanh_part)
    return (value * half, slope)


def conv_kernel(
    slots,
    field_ref,
    top_ref,
    bottom_ref,
    own_west,
    own_east,
    far_west,
    far_east,
    cot_hbm,
    forward_ref,
    backward_ref,
    pick_ref,
    act_hbm,
    grad_ref,
    reply_ref,
    rims,
    stack,
    dpre,
    cots,
    acts,
    side,
    dfield,
    packed,
    in_sem,
    out_sem,
    sem,
):
    step = pl.program_id(0)
    lane = lane_of((CP, PP))
    lane_wide = lane_of((CP, COLS))
    taps = 9 * CP

    def column(ref, at):
        return jnp.sum(jnp.where(lane == at, ref[0:CP, :].astype(F32), 0.0), axis=1, keepdims=True)

    def build(row):
        before = column(far_west, 32 + row)
        after = column(far_east, row)
        rows = rims[row]
        middle = rows.astype(F32)
        left = jnp.where(lane_wide == 0, before, pltpu.roll(middle, 1, 1))
        right = jnp.where(lane_wide == COLS - 1, after, pltpu.roll(middle, COLS - 1, 1))
        return jnp.concatenate([left.astype(BF16), rows, right.astype(BF16)], axis=0)

    def forward_rows():
        return [
            jnp.dot(
                forward_ref[...], stack[pl.ds(2 * step + i, 3)].reshape(taps, COLS), preferred_element_type=F32
            )
            for i in range(2)
        ]

    def finish_rows(pres):
        for i in range(2):
            p = 2 * step + i
            result, slope = gelu_parts(pres[i])
            acts[p] = result.astype(BF16)
            dpre[p] = (cots[p].astype(F32) * slope).astype(BF16)

    def next_rows():
        for i in range(2):
            row = 2 * step + 4 + i
            stack[row] = build(row)

    def backward_rows():
        first = 2 * (step - 2)
        outs = [
            jnp.dot(
                backward_ref[...], dpre[pl.ds(first + i, 3)].reshape(3 * HID, COLS), preferred_element_type=F32
            )
            for i in range(2)
        ]
        fields = [stack[pl.ds(first + 1 + i, 3)].reshape(taps, COLS) for i in range(2)]
        owns = [dpre[first + 1 + i] for i in range(2)]
        terms = lax.dot_general(
            jnp.concatenate(fields, axis=1),
            jnp.concatenate(owns, axis=1),
            (((1,), (1,)), ((), ())),
            preferred_element_type=F32,
        )
        return outs, terms

    def store_backward(outs, terms):
        grad_ref[0:taps, :] += terms
        quarters = COLS // PP
        for i in range(2):
            r = 2 * (step - 2) + i
            out = outs[i]
            after = jnp.sum(jnp.where(lane == 64 + r, side[0:CP, :], 0.0), axis=1, keepdims=True)
            before = jnp.sum(jnp.where(lane == r, side[2 * CP :, :], 0.0), axis=1, keepdims=True)
            rows = (
                jnp.where(lane_wide == COLS - 1, after, pltpu.roll(out[0:CP], COLS - 1, 1))
                + out[CP : 2 * CP]
                + jnp.where(lane_wide == 0, before, pltpu.roll(out[2 * CP :], 1, 1))
            )
            for q in range(quarters):
                at = pl.multiple_of((r * quarters + q) * CP, 8)
                dfield[pl.ds(at, CP), :] = rows[:, q * PP : (q + 1) * PP]

    def load(k):
        return pltpu.make_async_copy(cot_hbm.at[pl.ds(4 * k, 4)], cots.at[pl.ds(4 * k + 1, 4)], in_sem.at[k])

    def ship_act(k):
        return pltpu.make_async_copy(acts.at[pl.ds(4 * k + 1, 4)], act_hbm.at[pl.ds(4 * k, 4)], out_sem.at[k])

    @pl.when(step == 0)
    def _():
        for k in range(4):
            load(k).start()
        for i in range(2):
            rims[i] = top_ref[i * CP : (i + 1) * CP, :]
            rims[ROWS + 2 + i] = bottom_ref[i * CP : (i + 1) * CP, :]
        rims[2 : ROWS + 2] = field_ref[...]
        cots[0] = top_ref[2 * CP :, :]
        cots[ROWS + 1] = bottom_ref[2 * CP :, :]
        rims[ROWS + 4 : ROWS + 6] = jnp.zeros((2, CP, COLS), BF16)
        for row in range(4):
            stack[row] = build(row)
        grad_ref[...] = jnp.zeros(grad_ref.shape, F32)
        wests = [far_west[0:CP, :].astype(F32)] * 2 + [own_west[0:CP, :].astype(F32)]
        easts = [own_east[0:CP, :].astype(F32)] + [far_east[0:CP, :].astype(F32)] * 2
        west_at = (0, 32, 0)
        east_at = (32, 0, 32)
        parts = []
        for ky in range(3):
            for kx in range(3):
                w = pltpu.roll(wests[kx], (2 * PP - west_at[kx] - ky) % PP, 1)
                e = pltpu.roll(easts[kx], (2 * PP + 64 - east_at[kx] - ky) % PP, 1)
                parts.append(jnp.where(lane < 64, w, e))
        columns = jnp.concatenate(parts, axis=0).astype(BF16)
        pre = jnp.dot(forward_ref[...], columns, preferred_element_type=F32)
        unused, slope = gelu_parts(pre)
        cot_east = pltpu.roll(far_east[CP:, :].astype(F32), 64, 1)
        cot_cols = jnp.where(lane_of((HID, PP)) < 64, far_west[CP:, :].astype(F32), cot_east)
        dcol = (cot_cols * slope).astype(BF16).astype(F32)
        moved = [dcol] + [pltpu.roll(dcol, PP - m, 1) for m in (1, 2)]
        side[...] = jnp.dot(
            backward_ref[...], jnp.concatenate(moved, axis=0).astype(BF16), preferred_element_type=F32
        )
        load(0).wait()

    for k in (1, 2, 3):

        @pl.when(step == 2 * k)
        def _():
            load(k).wait()

    @pl.when(step < 2)
    def _():
        finish_rows(forward_rows())
        next_rows()

    @pl.when((step >= 2) & (step <= ROWS // 2))
    def _():
        outs, terms = backward_rows()
        pres = forward_rows()
        finish_rows(pres)
        next_rows()
        store_backward(outs, terms)

    @pl.when(step == ROWS // 2 + 1)
    def _():
        store_backward(*backward_rows())

    for k in range(4):

        @pl.when(step == 2 * k + 2)
        def _():
            ship_act(k).start()

    @pl.when(step == ROWS // 2 + 1)
    def _():
        devices = packed.shape[0]
        per = TILE // slots
        tiles = packed.shape[1] // TILE
        ships = sem.shape[0]
        cut = -(-tiles // (2 * ships)) * 2
        pick = pick_ref[...]

        def ship(k):
            rows = pl.ds(k * cut * TILE, (min(tiles, (k + 1) * cut) - k * cut) * TILE)
            return pltpu.make_async_copy(packed.at[:, rows, :], reply_ref.at[:, rows, :], sem.at[k])

        started = []
        for t in range(0, tiles, 2):
            pair = [t, t + 1] if t + 1 < tiles else [t]
            data = []
            for u in pair:
                chans = [
                    dfield[pl.ds(min(u * per + p, CP - 1), PIECES, stride=CP), :].astype(BF16) for p in range(per)
                ]
                data.append(jnp.concatenate(chans, axis=0) if per > 1 else chans[0])
            data = jnp.concatenate(data, axis=1) if len(data) > 1 else data[0]
            got = jnp.dot(pick, data, preferred_element_type=F32).astype(BF16)
            for n, u in enumerate(pair):
                packed[:, u * TILE : (u + 1) * TILE, :] = got[:, n * PP : (n + 1) * PP].reshape(devices, TILE, PP)
            if (t + 2) % cut == 0 or t + 2 >= tiles:
                k = t // cut
                ship(k).start()
                started.append(k)
        for k in range(4):
            ship_act(k).wait()
        for k in started:
            ship(k).wait()


def conv_call(slots, part, field, top, bottom, own_west, own_east, far_west, far_east, cot, forward, backward, pick):
    devices = pick.shape[0] // TILE
    reply_rows = part - TILE
    edges = [whole(x.shape) for x in (field, top, bottom, own_west, own_east, far_west, far_east)]
    return pl.pallas_call(
        functools.partial(conv_kernel, slots),
        grid=(ROWS // 2 + 2,),
        in_specs=edges
        + [anywhere()]
        + [whole(x.shape) for x in (forward, backward, pick)],
        out_specs=[anywhere(), whole((GRAD_ROWS, HID)), anywhere()],
        out_shape=[
            jax.ShapeDtypeStruct((ROWS, HID, COLS), BF16),
            jax.ShapeDtypeStruct((GRAD_ROWS, HID), F32),
            jax.ShapeDtypeStruct((devices, reply_rows, PP), BF16),
        ],
        scratch_shapes=[
            pltpu.VMEM((ROWS + 6, CP, COLS), BF16),
            pltpu.VMEM((ROWS + 6, 3 * CP, COLS), BF16),
            pltpu.VMEM((ROWS + 2, HID, COLS), BF16),
            pltpu.VMEM((ROWS + 2, HID, COLS), BF16),
            pltpu.VMEM((ROWS + 2, HID, COLS), BF16),
            pltpu.VMEM((3 * CP, PP), F32),
            pltpu.VMEM((PIECES * CP, PP), F32),
            pltpu.VMEM((devices, reply_rows, PP), BF16),
            pltpu.SemaphoreType.DMA((4,)),
            pltpu.SemaphoreType.DMA((4,)),
            pltpu.SemaphoreType.DMA((4,)),
        ],
        compiler_params=params(),
        name="conv_level",
    )(field, top, bottom, own_west, own_east, far_west, far_east, cot, forward, backward, pick)


def return_kernel(slots, devices, place_ref, back_hbm, weight_hbm, out_ref, back, weights, back_f, out_f, back_sem, in_sem):
    blocks = out_ref.shape[1]
    chunks = in_sem.shape[0]
    group = blocks // chunks
    cuts = back_sem.shape[0]
    size = back.shape[0] // cuts
    share = devices // cuts
    rows = back.shape[0] // devices
    part = rows + TILE
    trash = devices * part

    def fetch(k):
        span = pl.ds(k * size, size)
        return pltpu.make_async_copy(back_hbm.at[span], back.at[span], back_sem.at[k])

    def load(k):
        rows = pl.ds(k * group, group)
        return pltpu.make_async_copy(weight_hbm.at[rows], weights.at[rows], in_sem.at[k])

    for k in range(cuts):
        fetch(k).start()
    for k in range(chunks):
        load(k).start()

    def widen(k, carry):
        fetch(k).wait()
        for i in range(share):
            at = pl.multiple_of((k * share + i) * rows, TILE)
            to = pl.multiple_of((k * share + i) * part, TILE)
            back_f[pl.ds(to, rows), :] = back[pl.ds(at, rows), :].astype(F32)
        return carry

    lax.fori_loop(0, cuts, widen, 0)
    back_f[pl.ds(trash, CP * slots), :] = jnp.zeros((CP * slots, PP), F32)

    def gradients(k, carry):
        load(k).wait()
        for i in range(group):
            b = k * group + i
            total = jnp.zeros((C, PP), F32)
            for half in range(2):
                got = []
                for part_j in range(2):
                    at = place_ref[b * K + 2 * half + part_j]
                    got.append(back_f[pl.ds(at, C, stride=slots), :].astype(BF16))
                pair = jnp.concatenate([weights[b, 2 * half], weights[b, 2 * half + 1]], axis=1)
                total = total + lax.dot_general(
                    jnp.concatenate(got, axis=1), pair, (((1,), (1,)), ((), ())), preferred_element_type=F32
                )
            out_f[pl.ds(b, C, stride=blocks), :] = total
        return carry

    lax.fori_loop(0, chunks, gradients, 0)
    for c in range(C):
        out_ref[c] = out_f[c * blocks : (c + 1) * blocks, :].astype(BF16)


def return_call(place, back, weights, devices, slots):
    blocks = weights.shape[0]
    return pl.pallas_call(
        functools.partial(return_kernel, slots, devices),
        grid=(1,),
        in_specs=[smem(), anywhere(), anywhere()],
        out_specs=whole((C, blocks, PP)),
        out_shape=jax.ShapeDtypeStruct((C, blocks, PP), BF16),
        scratch_shapes=[
            pltpu.VMEM(back.shape, BF16),
            pltpu.VMEM(weights.shape, BF16),
            pltpu.VMEM((back.shape[0] + devices * TILE + CP * slots, PP), F32),
            pltpu.VMEM((CP * blocks, PP), F32),
            pltpu.SemaphoreType.DMA((8,)),
            pltpu.SemaphoreType.DMA((2,)),
        ],
        compiler_params=params(),
        name="block_gradients",
    )(place, back, weights)


def shift(value, face_by, tile_by):
    faces, tiles = lax.axis_size("face"), lax.axis_size("tile")
    pairs = [
        (f * tiles + t, (f + face_by) % faces * tiles + t + tile_by)
        for f in range(faces)
        for t in range(tiles)
        if 0 <= t + tile_by < tiles
    ]
    return lax.ppermute(value, BOTH, pairs)


def swap(value, axis, bit):
    return lax.ppermute(value, axis, [(i, i ^ (1 << bit)) for i in range(lax.axis_size(axis))])


def upper(axis, bit):
    return (lax.axis_index(axis) >> bit) & 1


def fold(value, axis, bit):
    half = value.shape[0] // 2
    mine = upper(axis, bit)
    keep = lax.dynamic_slice_in_dim(value, mine * half, half, axis=0)
    send = lax.dynamic_slice_in_dim(value, (1 - mine) * half, half, axis=0)
    return keep + swap(send, axis, bit)


def unfold(value, axis, bit):
    got = swap(value, axis, bit)
    first = upper(axis, bit) == 0
    return jnp.concatenate([jnp.where(first, value, got), jnp.where(first, got, value)], axis=0)


def local(latlon, intersection_weight, target_dev, target_piece, counts, conv_weight, cotangent):
    faces, tiles = lax.axis_size("face"), lax.axis_size("tile")
    devices = faces * tiles
    blocks = latlon.shape[0]
    slots = max(2, (blocks * K + devices - 1) // devices)
    part = -(-C * slots // TILE) * TILE + TILE

    lat = jnp.swapaxes(latlon, 0, 1)
    send, place = send_call(
        target_dev.T, target_piece.T, counts, lat, intersection_weight, devices, slots, part
    )
    recv = lax.all_to_all(send.reshape(devices, part, PP), BOTH, split_axis=0, concat_axis=0, tiled=True)

    forward, backward = taps_call(jnp.swapaxes(conv_weight, 1, 2))
    cot = jnp.swapaxes(cotangent[0], 0, 1)
    cot_first, cot_last = cotangent[0, :, 0, :], cotangent[0, :, ROWS - 1, :]
    cot_west = jnp.pad(cotangent[0, :, :, 0], ((0, 0), (1, PP - ROWS - 1)))
    cot_east = jnp.pad(cotangent[0, :, :, COLS - 1], ((0, 0), (1, PP - ROWS - 1)))
    recv, forward, backward, cot, cot_first, cot_last, cot_west, cot_east = lax.optimization_barrier(
        (recv, forward, backward, cot, cot_first, cot_last, cot_west, cot_east)
    )

    field, low, high, west, east, pick = gather_call(recv, cot_first, cot_last, slots)
    top = shift(high, 0, 1)
    bottom = shift(low, 0, -1)
    west, east = columns_call(west, east, cot_west, cot_east, top, bottom)
    far_west = shift(east, 1, 0)
    far_east = shift(west, -1, 0)
    act, grad, reply = conv_call(
        slots, part, field, top, bottom, west, east, far_west, far_east, cot, forward, backward, pick
    )
    activation = with_layout_constraint(jnp.swapaxes(act, 0, 1), Layout((0, 1, 2)))

    back = lax.all_to_all(reply, BOTH, split_axis=0, concat_axis=0, tiled=True)

    halves = [("tile", 0)] + [("face", bit) for bit in range((faces - 1).bit_length())]
    grad = fold(grad, *halves[0])
    grad, activation = lax.optimization_barrier((grad, activation))
    for axis, bit in halves[1:]:
        grad = fold(grad, axis, bit)
    groups = [list(range(first, tiles, 2)) for first in range(2)]
    grad = lax.psum(grad, "tile", axis_index_groups=groups)
    grad = grad * (1.0 / math.sqrt(devices * ROWS * COLS))
    for axis, bit in reversed(halves):
        grad = unfold(grad, axis, bit)
    grad_conv = jnp.swapaxes(grad[: 9 * CP].reshape(9, CP, HID)[:, :C, :], 1, 2)

    back = back.reshape(devices * (part - TILE), PP)
    grad_lat = return_call(place, back, intersection_weight, devices, slots)
    return (activation[None], grad_conv, jnp.swapaxes(grad_lat, 0, 1))


def solution(mesh):
    placed = (
        P(BOTH, None, None),
        P(BOTH, None, None, None),
        P(BOTH, None),
        P(BOTH, None),
        P(BOTH),
        P(),
        P("face", None, "tile", None),
    )
    return jax.shard_map(
        local,
        mesh=mesh,
        in_specs=placed,
        out_specs=(P("face", None, "tile", None), P(), P(BOTH, None, None)),
        check_vma=False,
    )
```

```python
import functools
import math

import jax
import jax.numpy as jnp
from jax import lax
from jax.experimental import pallas as pl
from jax.experimental.layout import Layout, with_layout_constraint
from jax.experimental.pallas import tpu as pltpu
from jax.sharding import PartitionSpec as P

C = 74
CP = 80
HID = 256
ROWS = 16
COLS = 512
PP = 128
K = 4
PIECES = 64
TILE = 16
GRAD_ROWS = 768
BOTH = ("face", "tile")
VMEM_LIMIT = 58 * 1024 * 1024
F32 = jnp.float32
BF16 = jnp.bfloat16


def params():
    return pltpu.CompilerParams(vmem_limit_bytes=VMEM_LIMIT)


def whole(shape):
    return pl.BlockSpec(shape, lambda *_: (0,) * len(shape))


def smem():
    return pl.BlockSpec(memory_space=pltpu.SMEM)


def send_kernel(
    slots, part, dev_ref, piece_ref, counts_ref, lat_hbm, weight_hbm, send_ref, place_ref, lat, weights, lat_f, store, packed, tally, lat_sem, in_sem, out_sem
):
    blocks = lat.shape[1]
    devices = send_ref.shape[0] // part
    trash = devices * part
    codes = part - TILE
    chunks = in_sem.shape[0]
    group = blocks // chunks
    ships = out_sem.shape[0]
    share = devices // ships

    def slot_of(rows):
        return lax.rem(lax.broadcasted_iota(jnp.int32, (rows, PP), 0), slots)

    def load(k):
        rows = pl.ds(k * group, group)
        return pltpu.make_async_copy(weight_hbm.at[rows], weights.at[rows], in_sem.at[k])

    def ship(k):
        rows = pl.ds(k * share * part, share * part)
        return pltpu.make_async_copy(packed.at[rows], send_ref.at[rows], out_sem.at[k])

    fetch = pltpu.make_async_copy(lat_hbm, lat, lat_sem)
    fetch.start()
    for k in range(chunks):
        load(k).start()

    def clear(d, carry):
        tally[d] = 0
        return carry

    lax.fori_loop(0, devices, clear, 0)

    def settle(b, carry):
        for j in range(K):
            live = j < counts_ref[b]
            d = dev_ref[j, b]
            s = tally[d]
            tally[d] = s + live.astype(jnp.int32)
            place_ref[b * K + j] = jnp.where(live, d * part + s, trash)
        return carry

    lax.fori_loop(0, blocks, settle, 0, unroll=4)
    fetch.wait()
    for c in range(C):
        lat_f[c * blocks : (c + 1) * blocks, :] = lat[c].astype(F32)

    def products(k, carry):
        load(k).wait()
        for i in range(group):
            b = k * group + i
            rows = lat_f[pl.ds(b, C, stride=blocks), :].astype(BF16)
            for half in range(2):
                pair = jnp.concatenate([weights[b, 2 * half], weights[b, 2 * half + 1]], axis=1)
                product = jnp.dot(rows, pair, preferred_element_type=F32)
                for part_j in range(2):
                    j = 2 * half + part_j
                    at = place_ref[b * K + j]
                    store[pl.ds(at, C, stride=slots), :] = product[:, part_j * PP : (part_j + 1) * PP]
                    code = jnp.full((TILE // slots, PP), piece_ref[j, b].astype(F32), F32)
                    store[pl.ds(at + codes, TILE // slots, stride=slots), :] = code
        return carry

    lax.fori_loop(0, chunks, products, 0)
    for k in range(ships):

        def pack(d, carry):
            used = tally[k * share + d]
            at = pl.multiple_of((k * share + d) * part, TILE)
            values = jnp.where(slot_of(codes) < used, store[pl.ds(at, codes), :], 0.0)
            packed[pl.ds(at, codes), :] = values.astype(BF16)
            subtiles = jnp.where(slot_of(TILE) < used, store[pl.ds(at + codes, TILE), :], -1.0)
            packed[pl.ds(at + codes, TILE), :] = subtiles.astype(BF16)
            return carry

        lax.fori_loop(0, share, pack, 0)
        ship(k).start()
    for k in range(ships):
        ship(k).wait()


def anywhere():
    return pl.BlockSpec(memory_space=pl.ANY)


def send_call(dev, piece, counts, lat, weights, devices, slots, part):
    blocks = lat.shape[1]
    return pl.pallas_call(
        functools.partial(send_kernel, slots, part),
        in_specs=[smem(), smem(), smem(), anywhere(), anywhere()],
        out_specs=[anywhere(), smem()],
        out_shape=[
            jax.ShapeDtypeStruct((devices * part, PP), BF16),
            jax.ShapeDtypeStruct((blocks * K,), jnp.int32),
        ],
        scratch_shapes=[
            pltpu.VMEM(lat.shape, BF16),
            pltpu.VMEM(weights.shape, BF16),
            pltpu.VMEM((CP * blocks, PP), F32),
            pltpu.VMEM((devices * part + part + CP * slots, PP), F32),
            pltpu.VMEM((devices * part, PP), BF16),
            pltpu.SMEM((devices,), jnp.int32),
            pltpu.SemaphoreType.DMA,
            pltpu.SemaphoreType.DMA((4,)),
            pltpu.SemaphoreType.DMA((8,)),
        ],
        compiler_params=params(),
        name="block_products",
    )(dev, piece, counts, lat, weights)


def lane_of(shape):
    return lax.broadcasted_iota(jnp.int32, shape, 1)


def put_columns(message, row, lane, first, second):
    message = jnp.where(lane == row, first, message)
    return jnp.where(lane == 32 + row, second, message)


def taps_kernel(weight_ref, forward_ref, backward_ref, taps):
    taps[...] = jnp.zeros(taps.shape, F32)
    for k in range(9):
        taps[k * CP : k * CP + C, :] = weight_ref[k].astype(F32)
    forward_ref[...] = jnp.transpose(taps[...]).astype(BF16)[:, 0 : 9 * CP]
    for m in range(3):
        rows = slice((2 - m) * 3 * CP, (3 - m) * 3 * CP)
        backward_ref[:, m * HID : (m + 1) * HID] = taps[rows, :].astype(BF16)


def taps_call(weight):
    return pl.pallas_call(
        taps_kernel,
        out_shape=[
            jax.ShapeDtypeStruct((HID, 9 * CP), BF16),
            jax.ShapeDtypeStruct((3 * CP, 3 * HID), BF16),
        ],
        scratch_shapes=[pltpu.VMEM((GRAD_ROWS, HID), F32)],
        name="taps",
    )(weight)


def gather_kernel(slots, recv_hbm, field_ref, low_ref, high_ref, west_ref, east_ref, pick_ref, recv_ref, total, sem):
    devices, part = recv_ref.shape[0], recv_ref.shape[1]
    per = TILE // slots
    tiles = part // TILE - 1
    keys = devices * TILE
    step = -(-tiles // 8) * 2
    cuts = list(range(0, tiles, step)) + [tiles]

    def load(k):
        first, end = (tiles, tiles + 1) if k == 0 else (cuts[k - 1], cuts[k])
        rows = pl.ds(first * TILE, (end - first) * TILE)
        return pltpu.make_async_copy(recv_hbm.at[:, rows, :], recv_ref.at[:, rows, :], sem.at[k])

    for k in range(len(cuts)):
        load(k).start()
    load(0).wait()
    codes = recv_ref[:, part - TILE :, :].astype(F32).reshape(keys, PP).astype(jnp.int32)
    within = lax.rem(lax.broadcasted_iota(jnp.int32, (keys, PP), 0), TILE)
    codes = jnp.where(codes < 0, -4096, codes + within // slots * PIECES)
    wide = per * PIECES
    picks = []
    for t in range(wide // PP):
        picks.append((codes == lane_of((keys, PP)) + t * PP).astype(F32))
    pick = jnp.concatenate(picks, axis=1) if len(picks) > 1 else picks[0]
    pick_ref[...] = pick.astype(BF16)
    pick_t = jnp.transpose(pick).astype(BF16)
    total[...] = jnp.zeros(total.shape, F32)
    for t in range(0, tiles, 2):
        if t in cuts:
            load(cuts.index(t) + 1).wait()
        pair = [t, t + 1] if t + 1 < tiles else [t]
        data = [recv_ref[:, u * TILE : (u + 1) * TILE, :].reshape(keys, PP) for u in pair]
        data = jnp.concatenate(data, axis=1) if len(data) > 1 else data[0]
        sums = jnp.dot(pick_t, data, preferred_element_type=F32)
        for n, u in enumerate(pair):
            for p in range(per):
                c = u * per + p
                if c < C:
                    total[pl.ds(c, PIECES, stride=CP), :] = sums[
                        p * PIECES : (p + 1) * PIECES, n * PP : (n + 1) * PP
                    ]
    lane = lane_of((CP, PP))
    west = jnp.zeros((CP, PP), F32)
    east = jnp.zeros((CP, PP), F32)
    quarters = COLS // PP
    for r in range(ROWS):
        for q in range(quarters):
            piece = r * quarters + q
            block = total[piece * CP : (piece + 1) * CP, :]
            out = block.astype(BF16)
            field_ref[r, :, q * PP : (q + 1) * PP] = out
            if r < 2:
                low_ref[r * CP : (r + 1) * CP, q * PP : (q + 1) * PP] = out
            if r >= ROWS - 2:
                high_ref[(r - ROWS + 2) * CP : (r - ROWS + 3) * CP, q * PP : (q + 1) * PP] = out
            if q == 0:
                west = put_columns(west, r + 2, lane, block[:, 0:1], block[:, 1:2])
            if q == quarters - 1:
                east = put_columns(east, r + 2, lane, block[:, PP - 2 : PP - 1], block[:, PP - 1 : PP])
    west_ref[...] = west.astype(BF16)
    east_ref[...] = east.astype(BF16)


def gather_call(recv, slots):
    devices = recv.shape[0]
    wide = TILE // slots * PIECES
    edge = (2 * CP, COLS)
    shapes = [(ROWS, CP, COLS), edge, edge, (CP, PP), (CP, PP), (devices * TILE, wide)]
    return pl.pallas_call(
        functools.partial(gather_kernel, slots),
        grid=(1,),
        in_specs=[anywhere()],
        out_specs=[whole(s) for s in shapes],
        out_shape=[jax.ShapeDtypeStruct(s, BF16) for s in shapes],
        scratch_shapes=[
            pltpu.VMEM(recv.shape, BF16),
            pltpu.VMEM((PIECES * CP, PP), F32),
            pltpu.SemaphoreType.DMA((8,)),
        ],
        compiler_params=params(),
        name="field_sum",
    )(recv)


def columns_kernel(west0, east0, cot_west, cot_east, top_ref, bottom_ref, cot_top, cot_bottom, west_ref, east_ref):
    lane = lane_of((CP, PP))
    west = west0[...].astype(F32)
    east = east0[...].astype(F32)
    for row, ref, i in ((0, top_ref, 0), (1, top_ref, 1), (ROWS + 2, bottom_ref, 0), (ROWS + 3, bottom_ref, 1)):
        left = ref[i * CP : (i + 1) * CP, 0:PP].astype(F32)
        right = ref[i * CP : (i + 1) * CP, COLS - PP : COLS].astype(F32)
        west = put_columns(west, row, lane, left[:, 0:1], left[:, 1:2])
        east = put_columns(east, row, lane, right[:, PP - 2 : PP - 1], right[:, PP - 1 : PP])
    west_ref[0:CP, :] = west.astype(BF16)
    east_ref[0:CP, :] = east.astype(BF16)
    lane = lane_of((HID, PP))
    west = cot_west[...].astype(F32)
    east = cot_east[...].astype(F32)
    for row, ref in ((0, cot_top), (ROWS + 1, cot_bottom)):
        west = jnp.where(lane == row, ref[:, 0:PP].astype(F32)[:, 0:1], west)
        east = jnp.where(lane == row, ref[:, COLS - PP : COLS].astype(F32)[:, PP - 1 : PP], east)
    west_ref[CP:, :] = west.astype(BF16)
    east_ref[CP:, :] = east.astype(BF16)


def columns_call(west, east, cot_west, cot_east, top, bottom, cot_top, cot_bottom):
    return pl.pallas_call(
        columns_kernel,
        out_shape=[jax.ShapeDtypeStruct((CP + HID, PP), BF16)] * 2,
        name="edge_columns",
    )(west, east, cot_west, cot_east, top, bottom, cot_top, cot_bottom)


def gelu_parts(value):
    square = value * value
    tanh_part = jnp.tanh(value * (0.7978845608 + (0.7978845608 * 0.044715) * square))
    half = 0.5 + 0.5 * tanh_part
    inner = (0.5 * 0.7978845608) + (0.5 * 0.7978845608 * 0.134145) * square
    slope = half + value * inner * (1.0 - tanh_part * tanh_part)
    return (value * half, slope)


def conv_kernel(
    slots,
    field_ref,
    top_ref,
    bottom_ref,
    own_west,
    own_east,
    far_west,
    far_east,
    cot_hbm,
    cot_top,
    cot_bottom,
    forward_ref,
    backward_ref,
    pick_ref,
    act_hbm,
    grad_ref,
    reply_ref,
    rims,
    stack,
    dpre,
    cots,
    acts,
    side,
    dfield,
    packed,
    in_sem,
    out_sem,
    sem,
):
    step = pl.program_id(0)
    lane = lane_of((CP, PP))
    lane_wide = lane_of((CP, COLS))
    taps = 9 * CP

    def column(ref, at):
        return jnp.sum(jnp.where(lane == at, ref[0:CP, :].astype(F32), 0.0), axis=1, keepdims=True)

    def build(row):
        before = column(far_west, 32 + row)
        after = column(far_east, row)
        rows = rims[row]
        middle = rows.astype(F32)
        left = jnp.where(lane_wide == 0, before, pltpu.roll(middle, 1, 1))
        right = jnp.where(lane_wide == COLS - 1, after, pltpu.roll(middle, COLS - 1, 1))
        return jnp.concatenate([left.astype(BF16), rows, right.astype(BF16)], axis=0)

    def forward_rows():
        return [
            jnp.dot(
                forward_ref[...], stack[pl.ds(2 * step + i, 3)].reshape(taps, COLS), preferred_element_type=F32
            )
            for i in range(2)
        ]

    def finish_rows(pres):
        for i in range(2):
            p = 2 * step + i
            result, slope = gelu_parts(pres[i])
            acts[p] = result.astype(BF16)
            dpre[p] = (cots[p].astype(F32) * slope).astype(BF16)

    def next_rows():
        for i in range(2):
            row = 2 * step + 4 + i
            stack[row] = build(row)

    def backward_rows():
        first = 2 * (step - 2)
        outs = [
            jnp.dot(
                backward_ref[...], dpre[pl.ds(first + i, 3)].reshape(3 * HID, COLS), preferred_element_type=F32
            )
            for i in range(2)
        ]
        fields = [stack[pl.ds(first + 1 + i, 3)].reshape(taps, COLS) for i in range(2)]
        owns = [dpre[first + 1 + i] for i in range(2)]
        terms = lax.dot_general(
            jnp.concatenate(fields, axis=1),
            jnp.concatenate(owns, axis=1),
            (((1,), (1,)), ((), ())),
            preferred_element_type=F32,
        )
        return outs, terms

    def store_backward(outs, terms):
        grad_ref[0:taps, :] += terms
        quarters = COLS // PP
        for i in range(2):
            r = 2 * (step - 2) + i
            out = outs[i]
            after = jnp.sum(jnp.where(lane == 64 + r, side[0:CP, :], 0.0), axis=1, keepdims=True)
            before = jnp.sum(jnp.where(lane == r, side[2 * CP :, :], 0.0), axis=1, keepdims=True)
            rows = (
                jnp.where(lane_wide == COLS - 1, after, pltpu.roll(out[0:CP], COLS - 1, 1))
                + out[CP : 2 * CP]
                + jnp.where(lane_wide == 0, before, pltpu.roll(out[2 * CP :], 1, 1))
            )
            for q in range(quarters):
                at = pl.multiple_of((r * quarters + q) * CP, 8)
                dfield[pl.ds(at, CP), :] = rows[:, q * PP : (q + 1) * PP]

    def load(k):
        return pltpu.make_async_copy(cot_hbm.at[pl.ds(4 * k, 4)], cots.at[pl.ds(4 * k + 1, 4)], in_sem.at[k])

    def ship_act(k):
        return pltpu.make_async_copy(acts.at[pl.ds(4 * k + 1, 4)], act_hbm.at[pl.ds(4 * k, 4)], out_sem.at[k])

    @pl.when(step == 0)
    def _():
        for k in range(4):
            load(k).start()
        for i in range(2):
            rims[i] = top_ref[i * CP : (i + 1) * CP, :]
            rims[ROWS + 2 + i] = bottom_ref[i * CP : (i + 1) * CP, :]
        rims[2 : ROWS + 2] = field_ref[...]
        cots[0] = cot_top[...]
        cots[ROWS + 1] = cot_bottom[...]
        rims[ROWS + 4 : ROWS + 6] = jnp.zeros((2, CP, COLS), BF16)
        for row in range(4):
            stack[row] = build(row)
        grad_ref[...] = jnp.zeros(grad_ref.shape, F32)
        wests = [far_west[0:CP, :].astype(F32)] * 2 + [own_west[0:CP, :].astype(F32)]
        easts = [own_east[0:CP, :].astype(F32)] + [far_east[0:CP, :].astype(F32)] * 2
        west_at = (0, 32, 0)
        east_at = (32, 0, 32)
        parts = []
        for ky in range(3):
            for kx in range(3):
                w = pltpu.roll(wests[kx], (2 * PP - west_at[kx] - ky) % PP, 1)
                e = pltpu.roll(easts[kx], (2 * PP + 64 - east_at[kx] - ky) % PP, 1)
                parts.append(jnp.where(lane < 64, w, e))
        columns = jnp.concatenate(parts, axis=0).astype(BF16)
        pre = jnp.dot(forward_ref[...], columns, preferred_element_type=F32)
        unused, slope = gelu_parts(pre)
        cot_east = pltpu.roll(far_east[CP:, :].astype(F32), 64, 1)
        cot_cols = jnp.where(lane_of((HID, PP)) < 64, far_west[CP:, :].astype(F32), cot_east)
        dcol = (cot_cols * slope).astype(BF16).astype(F32)
        moved = [dcol] + [pltpu.roll(dcol, PP - m, 1) for m in (1, 2)]
        side[...] = jnp.dot(
            backward_ref[...], jnp.concatenate(moved, axis=0).astype(BF16), preferred_element_type=F32
        )
        load(0).wait()

    for k in (1, 2, 3):

        @pl.when(step == 2 * k)
        def _():
            load(k).wait()

    @pl.when(step < 2)
    def _():
        finish_rows(forward_rows())
        next_rows()

    @pl.when((step >= 2) & (step <= ROWS // 2))
    def _():
        outs, terms = backward_rows()
        pres = forward_rows()
        finish_rows(pres)
        next_rows()
        store_backward(outs, terms)

    @pl.when(step == ROWS // 2 + 1)
    def _():
        store_backward(*backward_rows())

    for k in range(4):

        @pl.when(step == 2 * k + 2)
        def _():
            ship_act(k).start()

    @pl.when(step == ROWS // 2 + 1)
    def _():
        devices = packed.shape[0]
        per = TILE // slots
        tiles = packed.shape[1] // TILE
        ships = sem.shape[0]
        cut = -(-tiles // (2 * ships)) * 2
        pick = pick_ref[...]

        def ship(k):
            rows = pl.ds(k * cut * TILE, (min(tiles, (k + 1) * cut) - k * cut) * TILE)
            return pltpu.make_async_copy(packed.at[:, rows, :], reply_ref.at[:, rows, :], sem.at[k])

        started = []
        for t in range(0, tiles, 2):
            pair = [t, t + 1] if t + 1 < tiles else [t]
            data = []
            for u in pair:
                chans = [
                    dfield[pl.ds(min(u * per + p, CP - 1), PIECES, stride=CP), :].astype(BF16) for p in range(per)
                ]
                data.append(jnp.concatenate(chans, axis=0) if per > 1 else chans[0])
            data = jnp.concatenate(data, axis=1) if len(data) > 1 else data[0]
            got = jnp.dot(pick, data, preferred_element_type=F32).astype(BF16)
            for n, u in enumerate(pair):
                packed[:, u * TILE : (u + 1) * TILE, :] = got[:, n * PP : (n + 1) * PP].reshape(devices, TILE, PP)
            if (t + 2) % cut == 0 or t + 2 >= tiles:
                k = t // cut
                ship(k).start()
                started.append(k)
        for k in range(4):
            ship_act(k).wait()
        for k in started:
            ship(k).wait()


def conv_call(slots, part, field, top, bottom, own_west, own_east, far_west, far_east, cot, cot_top, cot_bottom, forward, backward, pick):
    devices = pick.shape[0] // TILE
    reply_rows = part - TILE
    edges = [whole(x.shape) for x in (field, top, bottom, own_west, own_east, far_west, far_east)]
    return pl.pallas_call(
        functools.partial(conv_kernel, slots),
        grid=(ROWS // 2 + 2,),
        in_specs=edges
        + [anywhere()]
        + [whole(x.shape) for x in (cot_top, cot_bottom, forward, backward, pick)],
        out_specs=[anywhere(), whole((GRAD_ROWS, HID)), anywhere()],
        out_shape=[
            jax.ShapeDtypeStruct((ROWS, HID, COLS), BF16),
            jax.ShapeDtypeStruct((GRAD_ROWS, HID), F32),
            jax.ShapeDtypeStruct((devices, reply_rows, PP), BF16),
        ],
        scratch_shapes=[
            pltpu.VMEM((ROWS + 6, CP, COLS), BF16),
            pltpu.VMEM((ROWS + 6, 3 * CP, COLS), BF16),
            pltpu.VMEM((ROWS + 2, HID, COLS), BF16),
            pltpu.VMEM((ROWS + 2, HID, COLS), BF16),
            pltpu.VMEM((ROWS + 2, HID, COLS), BF16),
            pltpu.VMEM((3 * CP, PP), F32),
            pltpu.VMEM((PIECES * CP, PP), F32),
            pltpu.VMEM((devices, reply_rows, PP), BF16),
            pltpu.SemaphoreType.DMA((4,)),
            pltpu.SemaphoreType.DMA((4,)),
            pltpu.SemaphoreType.DMA((4,)),
        ],
        compiler_params=params(),
        name="conv_level",
    )(field, top, bottom, own_west, own_east, far_west, far_east, cot, cot_top, cot_bottom, forward, backward, pick)


def return_kernel(slots, devices, place_ref, back_hbm, weight_hbm, out_ref, back, weights, back_f, out_f, back_sem, in_sem):
    blocks = out_ref.shape[1]
    chunks = in_sem.shape[0]
    group = blocks // chunks
    cuts = back_sem.shape[0]
    size = back.shape[0] // cuts
    share = devices // cuts
    rows = back.shape[0] // devices
    part = rows + TILE
    trash = devices * part

    def fetch(k):
        span = pl.ds(k * size, size)
        return pltpu.make_async_copy(back_hbm.at[span], back.at[span], back_sem.at[k])

    def load(k):
        rows = pl.ds(k * group, group)
        return pltpu.make_async_copy(weight_hbm.at[rows], weights.at[rows], in_sem.at[k])

    for k in range(cuts):
        fetch(k).start()
    for k in range(chunks):
        load(k).start()

    def widen(k, carry):
        fetch(k).wait()
        for i in range(share):
            at = pl.multiple_of((k * share + i) * rows, TILE)
            to = pl.multiple_of((k * share + i) * part, TILE)
            back_f[pl.ds(to, rows), :] = back[pl.ds(at, rows), :].astype(F32)
        return carry

    lax.fori_loop(0, cuts, widen, 0)
    back_f[pl.ds(trash, CP * slots), :] = jnp.zeros((CP * slots, PP), F32)

    def gradients(k, carry):
        load(k).wait()
        for i in range(group):
            b = k * group + i
            total = jnp.zeros((C, PP), F32)
            for half in range(2):
                got = []
                for part_j in range(2):
                    at = place_ref[b * K + 2 * half + part_j]
                    got.append(back_f[pl.ds(at, C, stride=slots), :].astype(BF16))
                pair = jnp.concatenate([weights[b, 2 * half], weights[b, 2 * half + 1]], axis=1)
                total = total + lax.dot_general(
                    jnp.concatenate(got, axis=1), pair, (((1,), (1,)), ((), ())), preferred_element_type=F32
                )
            out_f[pl.ds(b, C, stride=blocks), :] = total
        return carry

    lax.fori_loop(0, chunks, gradients, 0)
    for c in range(C):
        out_ref[c] = out_f[c * blocks : (c + 1) * blocks, :].astype(BF16)


def return_call(place, back, weights, devices, slots):
    blocks = weights.shape[0]
    return pl.pallas_call(
        functools.partial(return_kernel, slots, devices),
        grid=(1,),
        in_specs=[smem(), anywhere(), anywhere()],
        out_specs=whole((C, blocks, PP)),
        out_shape=jax.ShapeDtypeStruct((C, blocks, PP), BF16),
        scratch_shapes=[
            pltpu.VMEM(back.shape, BF16),
            pltpu.VMEM(weights.shape, BF16),
            pltpu.VMEM((back.shape[0] + devices * TILE + CP * slots, PP), F32),
            pltpu.VMEM((CP * blocks, PP), F32),
            pltpu.SemaphoreType.DMA((8,)),
            pltpu.SemaphoreType.DMA((2,)),
        ],
        compiler_params=params(),
        name="block_gradients",
    )(place, back, weights)


def shift(value, face_by, tile_by):
    faces, tiles = lax.axis_size("face"), lax.axis_size("tile")
    pairs = [
        (f * tiles + t, (f + face_by) % faces * tiles + t + tile_by)
        for f in range(faces)
        for t in range(tiles)
        if 0 <= t + tile_by < tiles
    ]
    return lax.ppermute(value, BOTH, pairs)


def swap(value, axis, bit):
    return lax.ppermute(value, axis, [(i, i ^ (1 << bit)) for i in range(lax.axis_size(axis))])


def upper(axis, bit):
    return (lax.axis_index(axis) >> bit) & 1


def fold(value, axis, bit):
    half = value.shape[0] // 2
    mine = upper(axis, bit)
    keep = lax.dynamic_slice_in_dim(value, mine * half, half, axis=0)
    send = lax.dynamic_slice_in_dim(value, (1 - mine) * half, half, axis=0)
    return keep + swap(send, axis, bit)


def unfold(value, axis, bit):
    got = swap(value, axis, bit)
    first = upper(axis, bit) == 0
    return jnp.concatenate([jnp.where(first, value, got), jnp.where(first, got, value)], axis=0)


def local(latlon, intersection_weight, target_dev, target_piece, counts, conv_weight, cotangent):
    faces, tiles = lax.axis_size("face"), lax.axis_size("tile")
    devices = faces * tiles
    blocks = latlon.shape[0]
    slots = max(2, (blocks * K + devices - 1) // devices)
    part = -(-C * slots // TILE) * TILE + TILE

    lat = jnp.swapaxes(latlon, 0, 1)
    send, place = send_call(
        target_dev.T, target_piece.T, counts, lat, intersection_weight, devices, slots, part
    )
    recv = lax.all_to_all(send.reshape(devices, part, PP), BOTH, split_axis=0, concat_axis=0, tiled=True)

    forward, backward = taps_call(jnp.swapaxes(conv_weight, 1, 2))
    cot = jnp.swapaxes(cotangent[0], 0, 1)
    cot_top = shift(cotangent[0, :, ROWS - 1, :], 0, 1)
    cot_bottom = shift(cotangent[0, :, 0, :], 0, -1)
    cot_west = jnp.pad(cotangent[0, :, :, 0], ((0, 0), (1, PP - ROWS - 1)))
    cot_east = jnp.pad(cotangent[0, :, :, COLS - 1], ((0, 0), (1, PP - ROWS - 1)))
    recv, forward, backward, cot, cot_west, cot_east = lax.optimization_barrier(
        (recv, forward, backward, cot, cot_west, cot_east)
    )

    field, low, high, west, east, pick = gather_call(recv, slots)
    top = shift(high, 0, 1)
    bottom = shift(low, 0, -1)
    west, east = columns_call(west, east, cot_west, cot_east, top, bottom, cot_top, cot_bottom)
    far_west = shift(east, 1, 0)
    far_east = shift(west, -1, 0)
    act, grad, reply = conv_call(
        slots, part, field, top, bottom, west, east, far_west, far_east, cot, cot_top, cot_bottom, forward, backward, pick
    )
    activation = with_layout_constraint(jnp.swapaxes(act, 0, 1), Layout((0, 1, 2)))

    back = lax.all_to_all(reply, BOTH, split_axis=0, concat_axis=0, tiled=True)

    halves = [("tile", 0)] + [("face", bit) for bit in range((faces - 1).bit_length())]
    grad = fold(grad, *halves[0])
    grad, activation = lax.optimization_barrier((grad, activation))
    for axis, bit in halves[1:]:
        grad = fold(grad, axis, bit)
    groups = [list(range(first, tiles, 2)) for first in range(2)]
    grad = lax.psum(grad, "tile", axis_index_groups=groups)
    grad = grad * (1.0 / math.sqrt(devices * ROWS * COLS))
    for axis, bit in reversed(halves):
        grad = unfold(grad, axis, bit)
    grad_conv = jnp.swapaxes(grad[: 9 * CP].reshape(9, CP, HID)[:, :C, :], 1, 2)

    back = back.reshape(devices * (part - TILE), PP)
    grad_lat = return_call(place, back, intersection_weight, devices, slots)
    return (activation[None], grad_conv, jnp.swapaxes(grad_lat, 0, 1))


def solution(mesh):
    placed = (
        P(BOTH, None, None),
        P(BOTH, None, None, None),
        P(BOTH, None),
        P(BOTH, None),
        P(BOTH),
        P(),
        P("face", None, "tile", None),
    )
    return jax.shard_map(
        local,
        mesh=mesh,
        in_specs=placed,
        out_specs=(P("face", None, "tile", None), P(), P(BOTH, None, None)),
        check_vma=False,
    )
```

```python
import functools
import math

import jax
import jax.numpy as jnp
from jax import lax
from jax.experimental import pallas as pl
from jax.experimental.layout import Layout, with_layout_constraint
from jax.experimental.pallas import tpu as pltpu
from jax.sharding import PartitionSpec as P

C = 74
CP = 80
HID = 256
ROWS = 16
COLS = 512
PP = 128
K = 4
PIECES = 64
TILE = 16
GRAD_ROWS = 768
BOTH = ("face", "tile")
VMEM_LIMIT = 58 * 1024 * 1024
F32 = jnp.float32
BF16 = jnp.bfloat16


def params():
    return pltpu.CompilerParams(vmem_limit_bytes=VMEM_LIMIT)


def whole(shape):
    return pl.BlockSpec(shape, lambda *_: (0,) * len(shape))


def smem():
    return pl.BlockSpec(memory_space=pltpu.SMEM)


def send_kernel(
    slots, part, dev_ref, piece_ref, counts_ref, lat_hbm, weight_hbm, send_ref, place_ref, lat, weights, lat_f, store, packed, tally, lat_sem, in_sem, out_sem
):
    blocks = lat.shape[1]
    devices = send_ref.shape[0] // part
    trash = devices * part
    codes = part - TILE
    chunks = in_sem.shape[0]
    group = blocks // chunks
    ships = out_sem.shape[0]
    share = devices // ships

    def slot_of(rows):
        return lax.rem(lax.broadcasted_iota(jnp.int32, (rows, PP), 0), slots)

    def load(k):
        rows = pl.ds(k * group, group)
        return pltpu.make_async_copy(weight_hbm.at[rows], weights.at[rows], in_sem.at[k])

    def ship(k):
        rows = pl.ds(k * share * part, share * part)
        return pltpu.make_async_copy(packed.at[rows], send_ref.at[rows], out_sem.at[k])

    fetch = pltpu.make_async_copy(lat_hbm, lat, lat_sem)
    fetch.start()
    for k in range(chunks):
        load(k).start()

    def clear(d, carry):
        tally[d] = 0
        return carry

    lax.fori_loop(0, devices, clear, 0)

    def settle(b, carry):
        for j in range(K):
            live = j < counts_ref[b]
            d = dev_ref[j, b]
            s = tally[d]
            tally[d] = s + live.astype(jnp.int32)
            place_ref[b * K + j] = jnp.where(live, d * part + s, trash)
        return carry

    lax.fori_loop(0, blocks, settle, 0, unroll=4)
    fetch.wait()
    for c in range(C):
        lat_f[c * blocks : (c + 1) * blocks, :] = lat[c].astype(F32)

    def products(k, carry):
        load(k).wait()
        for i in range(group):
            b = k * group + i
            rows = lat_f[pl.ds(b, C, stride=blocks), :].astype(BF16)
            for half in range(2):
                pair = jnp.concatenate([weights[b, 2 * half], weights[b, 2 * half + 1]], axis=1)
                product = jnp.dot(rows, pair, preferred_element_type=F32)
                for part_j in range(2):
                    j = 2 * half + part_j
                    at = place_ref[b * K + j]
                    store[pl.ds(at, C, stride=slots), :] = product[:, part_j * PP : (part_j + 1) * PP]
                    code = jnp.full((TILE // slots, PP), piece_ref[j, b].astype(F32), F32)
                    store[pl.ds(at + codes, TILE // slots, stride=slots), :] = code
        return carry

    lax.fori_loop(0, chunks, products, 0)
    for k in range(ships):

        def pack(d, carry):
            used = tally[k * share + d]
            at = pl.multiple_of((k * share + d) * part, TILE)
            values = jnp.where(slot_of(codes) < used, store[pl.ds(at, codes), :], 0.0)
            packed[pl.ds(at, codes), :] = values.astype(BF16)
            subtiles = jnp.where(slot_of(TILE) < used, store[pl.ds(at + codes, TILE), :], -1.0)
            packed[pl.ds(at + codes, TILE), :] = subtiles.astype(BF16)
            return carry

        lax.fori_loop(0, share, pack, 0)
        ship(k).start()
    for k in range(ships):
        ship(k).wait()


def anywhere():
    return pl.BlockSpec(memory_space=pl.ANY)


def send_call(dev, piece, counts, lat, weights, devices, slots, part):
    blocks = lat.shape[1]
    return pl.pallas_call(
        functools.partial(send_kernel, slots, part),
        in_specs=[smem(), smem(), smem(), anywhere(), anywhere()],
        out_specs=[anywhere(), smem()],
        out_shape=[
            jax.ShapeDtypeStruct((devices * part, PP), BF16),
            jax.ShapeDtypeStruct((blocks * K,), jnp.int32),
        ],
        scratch_shapes=[
            pltpu.VMEM(lat.shape, BF16),
            pltpu.VMEM(weights.shape, BF16),
            pltpu.VMEM((CP * blocks, PP), F32),
            pltpu.VMEM((devices * part + part + CP * slots, PP), F32),
            pltpu.VMEM((devices * part, PP), BF16),
            pltpu.SMEM((devices,), jnp.int32),
            pltpu.SemaphoreType.DMA,
            pltpu.SemaphoreType.DMA((2,)),
            pltpu.SemaphoreType.DMA((8,)),
        ],
        compiler_params=params(),
        name="block_products",
    )(dev, piece, counts, lat, weights)


def lane_of(shape):
    return lax.broadcasted_iota(jnp.int32, shape, 1)


def put_columns(message, row, lane, first, second):
    message = jnp.where(lane == row, first, message)
    return jnp.where(lane == 32 + row, second, message)


def taps_kernel(weight_ref, forward_ref, backward_ref, taps):
    taps[...] = jnp.zeros(taps.shape, F32)
    for k in range(9):
        taps[k * CP : k * CP + C, :] = weight_ref[k].astype(F32)
    forward_ref[...] = jnp.transpose(taps[...]).astype(BF16)[:, 0 : 9 * CP]
    for m in range(3):
        rows = slice((2 - m) * 3 * CP, (3 - m) * 3 * CP)
        backward_ref[:, m * HID : (m + 1) * HID] = taps[rows, :].astype(BF16)


def taps_call(weight):
    return pl.pallas_call(
        taps_kernel,
        out_shape=[
            jax.ShapeDtypeStruct((HID, 9 * CP), BF16),
            jax.ShapeDtypeStruct((3 * CP, 3 * HID), BF16),
        ],
        scratch_shapes=[pltpu.VMEM((GRAD_ROWS, HID), F32)],
        name="taps",
    )(weight)


def gather_kernel(slots, recv_hbm, field_ref, low_ref, high_ref, west_ref, east_ref, pick_ref, recv_ref, total, sem):
    devices, part = recv_ref.shape[0], recv_ref.shape[1]
    per = TILE // slots
    tiles = part // TILE - 1
    keys = devices * TILE
    step = -(-tiles // 8) * 2
    cuts = list(range(0, tiles, step)) + [tiles]

    def load(k):
        first, end = (tiles, tiles + 1) if k == 0 else (cuts[k - 1], cuts[k])
        rows = pl.ds(first * TILE, (end - first) * TILE)
        return pltpu.make_async_copy(recv_hbm.at[:, rows, :], recv_ref.at[:, rows, :], sem.at[k])

    for k in range(len(cuts)):
        load(k).start()
    load(0).wait()
    codes = recv_ref[:, part - TILE :, :].astype(F32).reshape(keys, PP).astype(jnp.int32)
    within = lax.rem(lax.broadcasted_iota(jnp.int32, (keys, PP), 0), TILE)
    codes = jnp.where(codes < 0, -4096, codes + within // slots * PIECES)
    wide = per * PIECES
    picks = []
    for t in range(wide // PP):
        picks.append((codes == lane_of((keys, PP)) + t * PP).astype(F32))
    pick = jnp.concatenate(picks, axis=1) if len(picks) > 1 else picks[0]
    pick_ref[...] = pick.astype(BF16)
    pick_t = jnp.transpose(pick).astype(BF16)
    total[...] = jnp.zeros(total.shape, F32)
    for t in range(0, tiles, 2):
        if t in cuts:
            load(cuts.index(t) + 1).wait()
        pair = [t, t + 1] if t + 1 < tiles else [t]
        data = [recv_ref[:, u * TILE : (u + 1) * TILE, :].reshape(keys, PP) for u in pair]
        data = jnp.concatenate(data, axis=1) if len(data) > 1 else data[0]
        sums = jnp.dot(pick_t, data, preferred_element_type=F32)
        for n, u in enumerate(pair):
            for p in range(per):
                c = u * per + p
                if c < C:
                    total[pl.ds(c, PIECES, stride=CP), :] = sums[
                        p * PIECES : (p + 1) * PIECES, n * PP : (n + 1) * PP
                    ]
    lane = lane_of((CP, PP))
    west = jnp.zeros((CP, PP), F32)
    east = jnp.zeros((CP, PP), F32)
    quarters = COLS // PP
    for r in range(ROWS):
        for q in range(quarters):
            piece = r * quarters + q
            block = total[piece * CP : (piece + 1) * CP, :]
            out = block.astype(BF16)
            field_ref[r, :, q * PP : (q + 1) * PP] = out
            if r < 2:
                low_ref[r * CP : (r + 1) * CP, q * PP : (q + 1) * PP] = out
            if r >= ROWS - 2:
                high_ref[(r - ROWS + 2) * CP : (r - ROWS + 3) * CP, q * PP : (q + 1) * PP] = out
            if q == 0:
                west = put_columns(west, r + 2, lane, block[:, 0:1], block[:, 1:2])
            if q == quarters - 1:
                east = put_columns(east, r + 2, lane, block[:, PP - 2 : PP - 1], block[:, PP - 1 : PP])
    west_ref[...] = west.astype(BF16)
    east_ref[...] = east.astype(BF16)


def gather_call(recv, slots):
    devices = recv.shape[0]
    wide = TILE // slots * PIECES
    edge = (2 * CP, COLS)
    shapes = [(ROWS, CP, COLS), edge, edge, (CP, PP), (CP, PP), (devices * TILE, wide)]
    return pl.pallas_call(
        functools.partial(gather_kernel, slots),
        grid=(1,),
        in_specs=[anywhere()],
        out_specs=[whole(s) for s in shapes],
        out_shape=[jax.ShapeDtypeStruct(s, BF16) for s in shapes],
        scratch_shapes=[
            pltpu.VMEM(recv.shape, BF16),
            pltpu.VMEM((PIECES * CP, PP), F32),
            pltpu.SemaphoreType.DMA((8,)),
        ],
        compiler_params=params(),
        name="field_sum",
    )(recv)


def columns_kernel(west0, east0, cot_west, cot_east, *refs):
    top_left, top_right, bottom_left, bottom_right = refs[0:4]
    cot_top_left, cot_top_right, cot_bottom_left, cot_bottom_right = refs[4:8]
    west_ref, east_ref = refs[8:]
    lane = lane_of((CP, PP))
    west = west0[...].astype(F32)
    east = east0[...].astype(F32)
    for first, left_ref, right_ref in ((0, top_left, top_right), (ROWS + 2, bottom_left, bottom_right)):
        for i in range(2):
            left = left_ref[i * CP : (i + 1) * CP, :].astype(F32)
            right = right_ref[i * CP : (i + 1) * CP, :].astype(F32)
            west = put_columns(west, first + i, lane, left[:, 0:1], left[:, 1:2])
            east = put_columns(east, first + i, lane, right[:, PP - 2 : PP - 1], right[:, PP - 1 : PP])
    west_ref[0:CP, :] = west.astype(BF16)
    east_ref[0:CP, :] = east.astype(BF16)
    lane = lane_of((HID, PP))
    west = cot_west[...].astype(F32)
    east = cot_east[...].astype(F32)
    for row, left_ref, right_ref in (
        (0, cot_top_left, cot_top_right),
        (ROWS + 1, cot_bottom_left, cot_bottom_right),
    ):
        west = jnp.where(lane == row, left_ref[...].astype(F32)[:, 0:1], west)
        east = jnp.where(lane == row, right_ref[...].astype(F32)[:, PP - 1 : PP], east)
    west_ref[CP:, :] = west.astype(BF16)
    east_ref[CP:, :] = east.astype(BF16)


def columns_call(west, east, cot_west, cot_east, *edges):
    ends = [pl.BlockSpec((x.shape[0], PP), lambda _, at=at: (0, at)) for x in edges for at in (0, COLS // PP - 1)]
    shape = (CP + HID, PP)
    return pl.pallas_call(
        columns_kernel,
        grid=(1,),
        in_specs=[whole(x.shape) for x in (west, east, cot_west, cot_east)] + ends,
        out_specs=[whole(shape)] * 2,
        out_shape=[jax.ShapeDtypeStruct(shape, BF16)] * 2,
        name="edge_columns",
    )(west, east, cot_west, cot_east, *[x for x in edges for _ in range(2)])


def gelu_parts(value):
    square = value * value
    tanh_part = jnp.tanh(value * (0.7978845608 + (0.7978845608 * 0.044715) * square))
    half = 0.5 + 0.5 * tanh_part
    inner = (0.5 * 0.7978845608) + (0.5 * 0.7978845608 * 0.134145) * square
    slope = half + value * inner * (1.0 - tanh_part * tanh_part)
    return (value * half, slope)


def conv_kernel(
    slots,
    field_ref,
    top_ref,
    bottom_ref,
    own_west,
    own_east,
    far_west,
    far_east,
    cot_hbm,
    cot_top,
    cot_bottom,
    forward_ref,
    backward_ref,
    pick_ref,
    act_hbm,
    grad_ref,
    reply_ref,
    rims,
    stack,
    dpre,
    cots,
    acts,
    side,
    dfield,
    packed,
    in_sem,
    out_sem,
    sem,
):
    step = pl.program_id(0)
    lane = lane_of((CP, PP))
    lane_wide = lane_of((CP, COLS))
    taps = 9 * CP

    def column(ref, at):
        return jnp.sum(jnp.where(lane == at, ref[0:CP, :].astype(F32), 0.0), axis=1, keepdims=True)

    def build(row):
        before = column(far_west, 32 + row)
        after = column(far_east, row)
        rows = rims[row]
        middle = rows.astype(F32)
        left = jnp.where(lane_wide == 0, before, pltpu.roll(middle, 1, 1))
        right = jnp.where(lane_wide == COLS - 1, after, pltpu.roll(middle, COLS - 1, 1))
        return jnp.concatenate([left.astype(BF16), rows, right.astype(BF16)], axis=0)

    def forward_rows():
        return [
            jnp.dot(
                forward_ref[...], stack[pl.ds(2 * step + i, 3)].reshape(taps, COLS), preferred_element_type=F32
            )
            for i in range(2)
        ]

    def finish_rows(pres):
        for i in range(2):
            p = 2 * step + i
            result, slope = gelu_parts(pres[i])
            acts[p] = result.astype(BF16)
            dpre[p] = (cots[p].astype(F32) * slope).astype(BF16)

    def next_rows():
        for i in range(2):
            row = 2 * step + 4 + i
            stack[row] = build(row)

    def backward_rows():
        first = 2 * (step - 2)
        outs = [
            jnp.dot(
                backward_ref[...], dpre[pl.ds(first + i, 3)].reshape(3 * HID, COLS), preferred_element_type=F32
            )
            for i in range(2)
        ]
        fields = [stack[pl.ds(first + 1 + i, 3)].reshape(taps, COLS) for i in range(2)]
        owns = [dpre[first + 1 + i] for i in range(2)]
        terms = lax.dot_general(
            jnp.concatenate(fields, axis=1),
            jnp.concatenate(owns, axis=1),
            (((1,), (1,)), ((), ())),
            preferred_element_type=F32,
        )
        return outs, terms

    def store_backward(outs, terms):
        grad_ref[0:taps, :] += terms
        quarters = COLS // PP
        for i in range(2):
            r = 2 * (step - 2) + i
            out = outs[i]
            after = jnp.sum(jnp.where(lane == 64 + r, side[0:CP, :], 0.0), axis=1, keepdims=True)
            before = jnp.sum(jnp.where(lane == r, side[2 * CP :, :], 0.0), axis=1, keepdims=True)
            rows = (
                jnp.where(lane_wide == COLS - 1, after, pltpu.roll(out[0:CP], COLS - 1, 1))
                + out[CP : 2 * CP]
                + jnp.where(lane_wide == 0, before, pltpu.roll(out[2 * CP :], 1, 1))
            )
            for q in range(quarters):
                at = pl.multiple_of((r * quarters + q) * CP, 8)
                dfield[pl.ds(at, CP), :] = rows[:, q * PP : (q + 1) * PP]

    def load(k):
        return pltpu.make_async_copy(cot_hbm.at[pl.ds(4 * k, 4)], cots.at[pl.ds(4 * k + 1, 4)], in_sem.at[k])

    def ship_act(k):
        return pltpu.make_async_copy(acts.at[pl.ds(4 * k + 1, 4)], act_hbm.at[pl.ds(4 * k, 4)], out_sem.at[k])

    @pl.when(step == 0)
    def _():
        for k in range(4):
            load(k).start()
        for i in range(2):
            rims[i] = top_ref[i * CP : (i + 1) * CP, :]
            rims[ROWS + 2 + i] = bottom_ref[i * CP : (i + 1) * CP, :]
        rims[2 : ROWS + 2] = field_ref[...]
        cots[0] = cot_top[...]
        cots[ROWS + 1] = cot_bottom[...]
        rims[ROWS + 4 : ROWS + 6] = jnp.zeros((2, CP, COLS), BF16)
        for row in range(4):
            stack[row] = build(row)
        grad_ref[...] = jnp.zeros(grad_ref.shape, F32)
        wests = [far_west[0:CP, :].astype(F32)] * 2 + [own_west[0:CP, :].astype(F32)]
        easts = [own_east[0:CP, :].astype(F32)] + [far_east[0:CP, :].astype(F32)] * 2
        west_at = (0, 32, 0)
        east_at = (32, 0, 32)
        parts = []
        for ky in range(3):
            for kx in range(3):
                w = pltpu.roll(wests[kx], (2 * PP - west_at[kx] - ky) % PP, 1)
                e = pltpu.roll(easts[kx], (2 * PP + 64 - east_at[kx] - ky) % PP, 1)
                parts.append(jnp.where(lane < 64, w, e))
        columns = jnp.concatenate(parts, axis=0).astype(BF16)
        pre = jnp.dot(forward_ref[...], columns, preferred_element_type=F32)
        unused, slope = gelu_parts(pre)
        cot_east = pltpu.roll(far_east[CP:, :].astype(F32), 64, 1)
        cot_cols = jnp.where(lane_of((HID, PP)) < 64, far_west[CP:, :].astype(F32), cot_east)
        dcol = (cot_cols * slope).astype(BF16).astype(F32)
        moved = [dcol] + [pltpu.roll(dcol, PP - m, 1) for m in (1, 2)]
        side[...] = jnp.dot(
            backward_ref[...], jnp.concatenate(moved, axis=0).astype(BF16), preferred_element_type=F32
        )
        load(0).wait()

    for k in (1, 2, 3):

        @pl.when(step == 2 * k)
        def _():
            load(k).wait()

    @pl.when(step < 2)
    def _():
        finish_rows(forward_rows())
        next_rows()

    @pl.when((step >= 2) & (step <= ROWS // 2))
    def _():
        outs, terms = backward_rows()
        pres = forward_rows()
        finish_rows(pres)
        next_rows()
        store_backward(outs, terms)

    @pl.when(step == ROWS // 2 + 1)
    def _():
        store_backward(*backward_rows())

    for k in range(4):

        @pl.when(step == 2 * k + 2)
        def _():
            ship_act(k).start()

    @pl.when(step == ROWS // 2 + 1)
    def _():
        devices = packed.shape[0]
        per = TILE // slots
        tiles = packed.shape[1] // TILE
        ships = sem.shape[0]
        cut = -(-tiles // (2 * ships)) * 2
        pick = pick_ref[...]

        def ship(k):
            rows = pl.ds(k * cut * TILE, (min(tiles, (k + 1) * cut) - k * cut) * TILE)
            return pltpu.make_async_copy(packed.at[:, rows, :], reply_ref.at[:, rows, :], sem.at[k])

        started = []
        for t in range(0, tiles, 2):
            pair = [t, t + 1] if t + 1 < tiles else [t]
            data = []
            for u in pair:
                chans = [
                    dfield[pl.ds(min(u * per + p, CP - 1), PIECES, stride=CP), :].astype(BF16) for p in range(per)
                ]
                data.append(jnp.concatenate(chans, axis=0) if per > 1 else chans[0])
            data = jnp.concatenate(data, axis=1) if len(data) > 1 else data[0]
            got = jnp.dot(pick, data, preferred_element_type=F32).astype(BF16)
            for n, u in enumerate(pair):
                packed[:, u * TILE : (u + 1) * TILE, :] = got[:, n * PP : (n + 1) * PP].reshape(devices, TILE, PP)
            if (t + 2) % cut == 0 or t + 2 >= tiles:
                k = t // cut
                ship(k).start()
                started.append(k)
        for k in range(4):
            ship_act(k).wait()
        for k in started:
            ship(k).wait()


def conv_call(slots, part, field, top, bottom, own_west, own_east, far_west, far_east, cot, cot_top, cot_bottom, forward, backward, pick):
    devices = pick.shape[0] // TILE
    reply_rows = part - TILE
    edges = [whole(x.shape) for x in (field, top, bottom, own_west, own_east, far_west, far_east)]
    return pl.pallas_call(
        functools.partial(conv_kernel, slots),
        grid=(ROWS // 2 + 2,),
        in_specs=edges
        + [anywhere()]
        + [whole(x.shape) for x in (cot_top, cot_bottom, forward, backward, pick)],
        out_specs=[anywhere(), whole((GRAD_ROWS, HID)), anywhere()],
        out_shape=[
            jax.ShapeDtypeStruct((ROWS, HID, COLS), BF16),
            jax.ShapeDtypeStruct((GRAD_ROWS, HID), F32),
            jax.ShapeDtypeStruct((devices, reply_rows, PP), BF16),
        ],
        scratch_shapes=[
            pltpu.VMEM((ROWS + 6, CP, COLS), BF16),
            pltpu.VMEM((ROWS + 6, 3 * CP, COLS), BF16),
            pltpu.VMEM((ROWS + 2, HID, COLS), BF16),
            pltpu.VMEM((ROWS + 2, HID, COLS), BF16),
            pltpu.VMEM((ROWS + 2, HID, COLS), BF16),
            pltpu.VMEM((3 * CP, PP), F32),
            pltpu.VMEM((PIECES * CP, PP), F32),
            pltpu.VMEM((devices, reply_rows, PP), BF16),
            pltpu.SemaphoreType.DMA((4,)),
            pltpu.SemaphoreType.DMA((4,)),
            pltpu.SemaphoreType.DMA((4,)),
        ],
        compiler_params=params(),
        name="conv_level",
    )(field, top, bottom, own_west, own_east, far_west, far_east, cot, cot_top, cot_bottom, forward, backward, pick)


def return_kernel(slots, devices, place_ref, back_hbm, weight_hbm, out_ref, back, weights, back_f, out_f, back_sem, in_sem):
    blocks = out_ref.shape[1]
    chunks = in_sem.shape[0]
    group = blocks // chunks
    cuts = back_sem.shape[0]
    size = back.shape[0] // cuts
    share = devices // cuts
    rows = back.shape[0] // devices
    part = rows + TILE
    trash = devices * part

    def fetch(k):
        span = pl.ds(k * size, size)
        return pltpu.make_async_copy(back_hbm.at[span], back.at[span], back_sem.at[k])

    def load(k):
        rows = pl.ds(k * group, group)
        return pltpu.make_async_copy(weight_hbm.at[rows], weights.at[rows], in_sem.at[k])

    for k in range(cuts):
        fetch(k).start()
    for k in range(chunks):
        load(k).start()

    def widen(k, carry):
        fetch(k).wait()
        for i in range(share):
            at = pl.multiple_of((k * share + i) * rows, TILE)
            to = pl.multiple_of((k * share + i) * part, TILE)
            back_f[pl.ds(to, rows), :] = back[pl.ds(at, rows), :].astype(F32)
        return carry

    lax.fori_loop(0, cuts, widen, 0)
    back_f[pl.ds(trash, CP * slots), :] = jnp.zeros((CP * slots, PP), F32)

    def gradients(k, carry):
        load(k).wait()
        for i in range(group):
            b = k * group + i
            total = jnp.zeros((C, PP), F32)
            for half in range(2):
                got = []
                for part_j in range(2):
                    at = place_ref[b * K + 2 * half + part_j]
                    got.append(back_f[pl.ds(at, C, stride=slots), :].astype(BF16))
                pair = jnp.concatenate([weights[b, 2 * half], weights[b, 2 * half + 1]], axis=1)
                total = total + lax.dot_general(
                    jnp.concatenate(got, axis=1), pair, (((1,), (1,)), ((), ())), preferred_element_type=F32
                )
            out_f[pl.ds(b, C, stride=blocks), :] = total
        return carry

    lax.fori_loop(0, chunks, gradients, 0)
    for c in range(C):
        out_ref[c] = out_f[c * blocks : (c + 1) * blocks, :].astype(BF16)


def return_call(place, back, weights, devices, slots):
    blocks = weights.shape[0]
    return pl.pallas_call(
        functools.partial(return_kernel, slots, devices),
        grid=(1,),
        in_specs=[smem(), anywhere(), anywhere()],
        out_specs=whole((C, blocks, PP)),
        out_shape=jax.ShapeDtypeStruct((C, blocks, PP), BF16),
        scratch_shapes=[
            pltpu.VMEM(back.shape, BF16),
            pltpu.VMEM(weights.shape, BF16),
            pltpu.VMEM((back.shape[0] + devices * TILE + CP * slots, PP), F32),
            pltpu.VMEM((CP * blocks, PP), F32),
            pltpu.SemaphoreType.DMA((8,)),
            pltpu.SemaphoreType.DMA((2,)),
        ],
        compiler_params=params(),
        name="block_gradients",
    )(place, back, weights)


def shift(value, face_by, tile_by):
    faces, tiles = lax.axis_size("face"), lax.axis_size("tile")
    pairs = [
        (f * tiles + t, (f + face_by) % faces * tiles + t + tile_by)
        for f in range(faces)
        for t in range(tiles)
        if 0 <= t + tile_by < tiles
    ]
    return lax.ppermute(value, BOTH, pairs)


def swap(value, axis, bit):
    return lax.ppermute(value, axis, [(i, i ^ (1 << bit)) for i in range(lax.axis_size(axis))])


def upper(axis, bit):
    return (lax.axis_index(axis) >> bit) & 1


def fold(value, axis, bit):
    half = value.shape[0] // 2
    mine = upper(axis, bit)
    keep = lax.dynamic_slice_in_dim(value, mine * half, half, axis=0)
    send = lax.dynamic_slice_in_dim(value, (1 - mine) * half, half, axis=0)
    return keep + swap(send, axis, bit)


def unfold(value, axis, bit):
    got = swap(value, axis, bit)
    first = upper(axis, bit) == 0
    return jnp.concatenate([jnp.where(first, value, got), jnp.where(first, got, value)], axis=0)


def local(latlon, intersection_weight, target_dev, target_piece, counts, conv_weight, cotangent):
    faces, tiles = lax.axis_size("face"), lax.axis_size("tile")
    devices = faces * tiles
    blocks = latlon.shape[0]
    slots = max(2, (blocks * K + devices - 1) // devices)
    part = -(-C * slots // TILE) * TILE + TILE

    lat = jnp.swapaxes(latlon, 0, 1)
    send, place = send_call(
        target_dev.T, target_piece.T, counts, lat, intersection_weight, devices, slots, part
    )
    recv = lax.all_to_all(send.reshape(devices, part, PP), BOTH, split_axis=0, concat_axis=0, tiled=True)

    forward, backward = taps_call(jnp.swapaxes(conv_weight, 1, 2))
    cot = jnp.swapaxes(cotangent[0], 0, 1)
    cot_top = shift(cotangent[0, :, ROWS - 1, :], 0, 1)
    cot_bottom = shift(cotangent[0, :, 0, :], 0, -1)
    cot_west = jnp.pad(cotangent[0, :, :, 0], ((0, 0), (1, PP - ROWS - 1)))
    cot_east = jnp.pad(cotangent[0, :, :, COLS - 1], ((0, 0), (1, PP - ROWS - 1)))
    recv, forward, backward, cot, cot_west, cot_east = lax.optimization_barrier(
        (recv, forward, backward, cot, cot_west, cot_east)
    )

    field, low, high, west, east, pick = gather_call(recv, slots)
    top = shift(high, 0, 1)
    bottom = shift(low, 0, -1)
    west, east = columns_call(west, east, cot_west, cot_east, top, bottom, cot_top, cot_bottom)
    far_west = shift(east, 1, 0)
    far_east = shift(west, -1, 0)
    act, grad, reply = conv_call(
        slots, part, field, top, bottom, west, east, far_west, far_east, cot, cot_top, cot_bottom, forward, backward, pick
    )
    activation = with_layout_constraint(jnp.swapaxes(act, 0, 1), Layout((0, 1, 2)))

    back = lax.all_to_all(reply, BOTH, split_axis=0, concat_axis=0, tiled=True)

    halves = [("tile", 0)] + [("face", bit) for bit in range((faces - 1).bit_length())]
    grad = fold(grad, *halves[0])
    grad, activation = lax.optimization_barrier((grad, activation))
    for axis, bit in halves[1:]:
        grad = fold(grad, axis, bit)
    groups = [list(range(first, tiles, 2)) for first in range(2)]
    grad = lax.psum(grad, "tile", axis_index_groups=groups)
    grad = grad * (1.0 / math.sqrt(devices * ROWS * COLS))
    for axis, bit in reversed(halves):
        grad = unfold(grad, axis, bit)
    grad_conv = jnp.swapaxes(grad[: 9 * CP].reshape(9, CP, HID)[:, :C, :], 1, 2)

    back = back.reshape(devices * (part - TILE), PP)
    grad_lat = return_call(place, back, intersection_weight, devices, slots)
    return (activation[None], grad_conv, jnp.swapaxes(grad_lat, 0, 1))


def solution(mesh):
    placed = (
        P(BOTH, None, None),
        P(BOTH, None, None, None),
        P(BOTH, None),
        P(BOTH, None),
        P(BOTH),
        P(),
        P("face", None, "tile", None),
    )
    return jax.shard_map(
        local,
        mesh=mesh,
        in_specs=placed,
        out_specs=(P("face", None, "tile", None), P(), P(BOTH, None, None)),
        check_vma=False,
    )
```

```python
import functools
import math

import jax
import jax.numpy as jnp
from jax import lax
from jax.experimental import pallas as pl
from jax.experimental.layout import Layout, with_layout_constraint
from jax.experimental.pallas import tpu as pltpu
from jax.sharding import PartitionSpec as P

C = 74
CP = 80
HID = 256
ROWS = 16
COLS = 512
PP = 128
K = 4
PIECES = 64
TILE = 16
GRAD_ROWS = 768
BOTH = ("face", "tile")
VMEM_LIMIT = 58 * 1024 * 1024
F32 = jnp.float32
BF16 = jnp.bfloat16


def params():
    return pltpu.CompilerParams(vmem_limit_bytes=VMEM_LIMIT)


def whole(shape):
    return pl.BlockSpec(shape, lambda *_: (0,) * len(shape))


def smem():
    return pl.BlockSpec(memory_space=pltpu.SMEM)


def send_kernel(
    slots, part, dev_ref, piece_ref, counts_ref, lat_hbm, weight_hbm, send_ref, place_ref, lat, weights, lat_f, store, packed, tally, lat_sem, in_sem, out_sem
):
    blocks = lat.shape[1]
    devices = send_ref.shape[0] // part
    trash = devices * part
    codes = part - TILE
    chunks = in_sem.shape[0]
    group = blocks // chunks
    ships = out_sem.shape[0]
    share = devices // ships

    def slot_of(rows):
        return lax.rem(lax.broadcasted_iota(jnp.int32, (rows, PP), 0), slots)

    def load(k):
        rows = pl.ds(k * group, group)
        return pltpu.make_async_copy(weight_hbm.at[rows], weights.at[rows], in_sem.at[k])

    def ship(k):
        rows = pl.ds(k * share * part, share * part)
        return pltpu.make_async_copy(packed.at[rows], send_ref.at[rows], out_sem.at[k])

    fetch = pltpu.make_async_copy(lat_hbm, lat, lat_sem)
    fetch.start()
    for k in range(chunks):
        load(k).start()

    def clear(d, carry):
        tally[d] = 0
        return carry

    lax.fori_loop(0, devices, clear, 0)

    def settle(b, carry):
        for j in range(K):
            live = j < counts_ref[b]
            d = dev_ref[j, b]
            s = tally[d]
            tally[d] = s + live.astype(jnp.int32)
            place_ref[b * K + j] = jnp.where(live, d * part + s, trash)
        return carry

    lax.fori_loop(0, blocks, settle, 0, unroll=4)
    fetch.wait()
    for c in range(C):
        lat_f[c * blocks : (c + 1) * blocks, :] = lat[c].astype(F32)

    def products(k, carry):
        load(k).wait()
        for i in range(group):
            b = k * group + i
            rows = lat_f[pl.ds(b, C, stride=blocks), :].astype(BF16)
            for half in range(2):
                pair = jnp.concatenate([weights[b, 2 * half], weights[b, 2 * half + 1]], axis=1)
                product = jnp.dot(rows, pair, preferred_element_type=F32)
                for part_j in range(2):
                    j = 2 * half + part_j
                    at = place_ref[b * K + j]
                    store[pl.ds(at, C, stride=slots), :] = product[:, part_j * PP : (part_j + 1) * PP]
                    code = jnp.full((TILE // slots, PP), piece_ref[j, b].astype(F32), F32)
                    store[pl.ds(at + codes, TILE // slots, stride=slots), :] = code
        return carry

    lax.fori_loop(0, chunks, products, 0)
    for k in range(ships):

        def pack(d, carry):
            used = tally[k * share + d]
            at = pl.multiple_of((k * share + d) * part, TILE)
            filled = slot_of(codes) < used
            if codes > C * slots:
                filled = filled & (lax.broadcasted_iota(jnp.int32, (codes, PP), 0) < C * slots)
            values = jnp.where(filled, store[pl.ds(at, codes), :], 0.0)
            packed[pl.ds(at, codes), :] = values.astype(BF16)
            subtiles = jnp.where(slot_of(TILE) < used, store[pl.ds(at + codes, TILE), :], -1.0)
            packed[pl.ds(at + codes, TILE), :] = subtiles.astype(BF16)
            return carry

        lax.fori_loop(0, share, pack, 0)
        ship(k).start()
    for k in range(ships):
        ship(k).wait()


def anywhere():
    return pl.BlockSpec(memory_space=pl.ANY)


def send_call(dev, piece, counts, lat, weights, devices, slots, part):
    blocks = lat.shape[1]
    return pl.pallas_call(
        functools.partial(send_kernel, slots, part),
        in_specs=[smem(), smem(), smem(), anywhere(), anywhere()],
        out_specs=[anywhere(), smem()],
        out_shape=[
            jax.ShapeDtypeStruct((devices * part, PP), BF16),
            jax.ShapeDtypeStruct((blocks * K,), jnp.int32),
        ],
        scratch_shapes=[
            pltpu.VMEM(lat.shape, BF16),
            pltpu.VMEM(weights.shape, BF16),
            pltpu.VMEM((CP * blocks, PP), F32),
            pltpu.VMEM((devices * part + part + CP * slots, PP), F32),
            pltpu.VMEM((devices * part, PP), BF16),
            pltpu.SMEM((devices,), jnp.int32),
            pltpu.SemaphoreType.DMA,
            pltpu.SemaphoreType.DMA((2,)),
            pltpu.SemaphoreType.DMA((8,)),
        ],
        compiler_params=params(),
        name="block_products",
    )(dev, piece, counts, lat, weights)


def lane_of(shape):
    return lax.broadcasted_iota(jnp.int32, shape, 1)


def put_columns(message, row, lane, first, second):
    message = jnp.where(lane == row, first, message)
    return jnp.where(lane == 32 + row, second, message)


def taps_kernel(weight_ref, forward_ref, backward_ref, taps):
    taps[...] = jnp.zeros(taps.shape, F32)
    for k in range(9):
        taps[k * CP : k * CP + C, :] = weight_ref[k].astype(F32)
    forward_ref[...] = jnp.transpose(taps[...]).astype(BF16)[:, 0 : 9 * CP]
    for m in range(3):
        rows = slice((2 - m) * 3 * CP, (3 - m) * 3 * CP)
        backward_ref[:, m * HID : (m + 1) * HID] = taps[rows, :].astype(BF16)


def taps_call(weight):
    return pl.pallas_call(
        taps_kernel,
        out_shape=[
            jax.ShapeDtypeStruct((HID, 9 * CP), BF16),
            jax.ShapeDtypeStruct((3 * CP, 3 * HID), BF16),
        ],
        scratch_shapes=[pltpu.VMEM((GRAD_ROWS, HID), F32)],
        name="taps",
    )(weight)


def gather_kernel(slots, recv_hbm, field_ref, low_ref, high_ref, west_ref, east_ref, pick_ref, recv_ref, total, sem):
    devices, part = recv_ref.shape[0], recv_ref.shape[1]
    per = TILE // slots
    tiles = part // TILE - 1
    keys = devices * TILE
    step = -(-tiles // 8) * 2
    cuts = list(range(0, tiles, step)) + [tiles]

    def load(k):
        first, end = (tiles, tiles + 1) if k == 0 else (cuts[k - 1], cuts[k])
        rows = pl.ds(first * TILE, (end - first) * TILE)
        return pltpu.make_async_copy(recv_hbm.at[:, rows, :], recv_ref.at[:, rows, :], sem.at[k])

    for k in range(len(cuts)):
        load(k).start()
    load(0).wait()
    codes = recv_ref[:, part - TILE :, :].astype(F32).reshape(keys, PP).astype(jnp.int32)
    within = lax.rem(lax.broadcasted_iota(jnp.int32, (keys, PP), 0), TILE)
    codes = jnp.where(codes < 0, -4096, codes + within // slots * PIECES)
    wide = per * PIECES
    picks = []
    for t in range(wide // PP):
        picks.append((codes == lane_of((keys, PP)) + t * PP).astype(F32))
    pick = jnp.concatenate(picks, axis=1) if len(picks) > 1 else picks[0]
    pick_ref[...] = pick.astype(BF16)
    pick_t = jnp.transpose(pick).astype(BF16)
    total[...] = jnp.zeros(total.shape, F32)
    for t in range(0, tiles, 2):
        if t in cuts:
            load(cuts.index(t) + 1).wait()
        pair = [t, t + 1] if t + 1 < tiles else [t]
        data = [recv_ref[:, u * TILE : (u + 1) * TILE, :].reshape(keys, PP) for u in pair]
        data = jnp.concatenate(data, axis=1) if len(data) > 1 else data[0]
        sums = jnp.dot(pick_t, data, preferred_element_type=F32)
        for n, u in enumerate(pair):
            for p in range(per):
                c = u * per + p
                if c < C:
                    total[pl.ds(c, PIECES, stride=CP), :] = sums[
                        p * PIECES : (p + 1) * PIECES, n * PP : (n + 1) * PP
                    ]
    lane = lane_of((CP, PP))
    west = jnp.zeros((CP, PP), F32)
    east = jnp.zeros((CP, PP), F32)
    quarters = COLS // PP
    for r in range(ROWS):
        for q in range(quarters):
            piece = r * quarters + q
            block = total[piece * CP : (piece + 1) * CP, :]
            out = block.astype(BF16)
            field_ref[r, :, q * PP : (q + 1) * PP] = out
            if r < 2:
                low_ref[r * CP : (r + 1) * CP, q * PP : (q + 1) * PP] = out
            if r >= ROWS - 2:
                high_ref[(r - ROWS + 2) * CP : (r - ROWS + 3) * CP, q * PP : (q + 1) * PP] = out
            if q == 0:
                west = put_columns(west, r + 2, lane, block[:, 0:1], block[:, 1:2])
            if q == quarters - 1:
                east = put_columns(east, r + 2, lane, block[:, PP - 2 : PP - 1], block[:, PP - 1 : PP])
    west_ref[...] = west.astype(BF16)
    east_ref[...] = east.astype(BF16)


def gather_call(recv, slots):
    devices = recv.shape[0]
    wide = TILE // slots * PIECES
    edge = (2 * CP, COLS)
    shapes = [(ROWS, CP, COLS), edge, edge, (CP, PP), (CP, PP), (devices * TILE, wide)]
    return pl.pallas_call(
        functools.partial(gather_kernel, slots),
        grid=(1,),
        in_specs=[anywhere()],
        out_specs=[whole(s) for s in shapes],
        out_shape=[jax.ShapeDtypeStruct(s, BF16) for s in shapes],
        scratch_shapes=[
            pltpu.VMEM(recv.shape, BF16),
            pltpu.VMEM((PIECES * CP, PP), F32),
            pltpu.SemaphoreType.DMA((8,)),
        ],
        compiler_params=params(),
        name="field_sum",
    )(recv)


def columns_kernel(west0, east0, cot_west, cot_east, *refs):
    top_left, top_right, bottom_left, bottom_right = refs[0:4]
    cot_top_left, cot_top_right, cot_bottom_left, cot_bottom_right = refs[4:8]
    west_ref, east_ref = refs[8:]
    lane = lane_of((CP, PP))
    west = west0[...].astype(F32)
    east = east0[...].astype(F32)
    for first, left_ref, right_ref in ((0, top_left, top_right), (ROWS + 2, bottom_left, bottom_right)):
        for i in range(2):
            left = left_ref[i * CP : (i + 1) * CP, :].astype(F32)
            right = right_ref[i * CP : (i + 1) * CP, :].astype(F32)
            west = put_columns(west, first + i, lane, left[:, 0:1], left[:, 1:2])
            east = put_columns(east, first + i, lane, right[:, PP - 2 : PP - 1], right[:, PP - 1 : PP])
    west_ref[0:CP, :] = west.astype(BF16)
    east_ref[0:CP, :] = east.astype(BF16)
    lane = lane_of((HID, PP))
    west = cot_west[...].astype(F32)
    east = cot_east[...].astype(F32)
    for row, left_ref, right_ref in (
        (0, cot_top_left, cot_top_right),
        (ROWS + 1, cot_bottom_left, cot_bottom_right),
    ):
        west = jnp.where(lane == row, left_ref[...].astype(F32)[:, 0:1], west)
        east = jnp.where(lane == row, right_ref[...].astype(F32)[:, PP - 1 : PP], east)
    west_ref[CP:, :] = west.astype(BF16)
    east_ref[CP:, :] = east.astype(BF16)


def columns_call(west, east, cot_west, cot_east, *edges):
    ends = [pl.BlockSpec((x.shape[0], PP), lambda _, at=at: (0, at)) for x in edges for at in (0, COLS // PP - 1)]
    shape = (CP + HID, PP)
    return pl.pallas_call(
        columns_kernel,
        grid=(1,),
        in_specs=[whole(x.shape) for x in (west, east, cot_west, cot_east)] + ends,
        out_specs=[whole(shape)] * 2,
        out_shape=[jax.ShapeDtypeStruct(shape, BF16)] * 2,
        name="edge_columns",
    )(west, east, cot_west, cot_east, *[x for x in edges for _ in range(2)])


def gelu_parts(value):
    square = value * value
    tanh_part = jnp.tanh(value * (0.7978845608 + (0.7978845608 * 0.044715) * square))
    half = 0.5 + 0.5 * tanh_part
    inner = (0.5 * 0.7978845608) + (0.5 * 0.7978845608 * 0.134145) * square
    slope = half + value * inner * (1.0 - tanh_part * tanh_part)
    return (value * half, slope)


def conv_kernel(
    slots,
    field_ref,
    top_ref,
    bottom_ref,
    own_west,
    own_east,
    far_west,
    far_east,
    cot_hbm,
    cot_top,
    cot_bottom,
    forward_ref,
    backward_ref,
    pick_ref,
    act_hbm,
    grad_ref,
    reply_ref,
    rims,
    stack,
    dpre,
    cots,
    acts,
    side,
    dfield,
    packed,
    in_sem,
    out_sem,
    sem,
):
    step = pl.program_id(0)
    lane = lane_of((CP, PP))
    lane_wide = lane_of((CP, COLS))
    taps = 9 * CP

    def column(ref, at):
        return jnp.sum(jnp.where(lane == at, ref[0:CP, :].astype(F32), 0.0), axis=1, keepdims=True)

    def build(row):
        before = column(far_west, 32 + row)
        after = column(far_east, row)
        rows = rims[row]
        middle = rows.astype(F32)
        left = jnp.where(lane_wide == 0, before, pltpu.roll(middle, 1, 1))
        right = jnp.where(lane_wide == COLS - 1, after, pltpu.roll(middle, COLS - 1, 1))
        return jnp.concatenate([left.astype(BF16), rows, right.astype(BF16)], axis=0)

    def forward_rows():
        return [
            jnp.dot(
                forward_ref[...], stack[pl.ds(2 * step + i, 3)].reshape(taps, COLS), preferred_element_type=F32
            )
            for i in range(2)
        ]

    def finish_rows(pres):
        for i in range(2):
            p = 2 * step + i
            result, slope = gelu_parts(pres[i])
            acts[p] = result.astype(BF16)
            dpre[p] = (cots[p].astype(F32) * slope).astype(BF16)

    def next_rows():
        for i in range(2):
            row = 2 * step + 4 + i
            stack[row] = build(row)

    def backward_rows():
        first = 2 * (step - 2)
        outs = [
            jnp.dot(
                backward_ref[...], dpre[pl.ds(first + i, 3)].reshape(3 * HID, COLS), preferred_element_type=F32
            )
            for i in range(2)
        ]
        fields = [stack[pl.ds(first + 1 + i, 3)].reshape(taps, COLS) for i in range(2)]
        owns = [dpre[first + 1 + i] for i in range(2)]
        terms = lax.dot_general(
            jnp.concatenate(fields, axis=1),
            jnp.concatenate(owns, axis=1),
            (((1,), (1,)), ((), ())),
            preferred_element_type=F32,
        )
        return outs, terms

    def store_backward(outs, terms):
        grad_ref[0:taps, :] += terms
        quarters = COLS // PP
        for i in range(2):
            r = 2 * (step - 2) + i
            out = outs[i]
            after = jnp.sum(jnp.where(lane == 64 + r, side[0:CP, :], 0.0), axis=1, keepdims=True)
            before = jnp.sum(jnp.where(lane == r, side[2 * CP :, :], 0.0), axis=1, keepdims=True)
            rows = (
                jnp.where(lane_wide == COLS - 1, after, pltpu.roll(out[0:CP], COLS - 1, 1))
                + out[CP : 2 * CP]
                + jnp.where(lane_wide == 0, before, pltpu.roll(out[2 * CP :], 1, 1))
            )
            for q in range(quarters):
                at = pl.multiple_of((r * quarters + q) * CP, 8)
                dfield[pl.ds(at, CP), :] = rows[:, q * PP : (q + 1) * PP]

    def load(k):
        return pltpu.make_async_copy(cot_hbm.at[pl.ds(4 * k, 4)], cots.at[pl.ds(4 * k + 1, 4)], in_sem.at[k])

    def ship_act(k):
        return pltpu.make_async_copy(acts.at[pl.ds(4 * k + 1, 4)], act_hbm.at[pl.ds(4 * k, 4)], out_sem.at[k])

    @pl.when(step == 0)
    def _():
        for k in range(4):
            load(k).start()
        for i in range(2):
            rims[i] = top_ref[i * CP : (i + 1) * CP, :]
            rims[ROWS + 2 + i] = bottom_ref[i * CP : (i + 1) * CP, :]
        rims[2 : ROWS + 2] = field_ref[...]
        cots[0] = cot_top[...]
        cots[ROWS + 1] = cot_bottom[...]
        rims[ROWS + 4 : ROWS + 6] = jnp.zeros((2, CP, COLS), BF16)
        for row in range(4):
            stack[row] = build(row)
        grad_ref[...] = jnp.zeros(grad_ref.shape, F32)
        wests = [far_west[0:CP, :].astype(F32)] * 2 + [own_west[0:CP, :].astype(F32)]
        easts = [own_east[0:CP, :].astype(F32)] + [far_east[0:CP, :].astype(F32)] * 2
        west_at = (0, 32, 0)
        east_at = (32, 0, 32)
        parts = []
        for ky in range(3):
            for kx in range(3):
                w = pltpu.roll(wests[kx], (2 * PP - west_at[kx] - ky) % PP, 1)
                e = pltpu.roll(easts[kx], (2 * PP + 64 - east_at[kx] - ky) % PP, 1)
                parts.append(jnp.where(lane < 64, w, e))
        columns = jnp.concatenate(parts, axis=0).astype(BF16)
        pre = jnp.dot(forward_ref[...], columns, preferred_element_type=F32)
        unused, slope = gelu_parts(pre)
        cot_east = pltpu.roll(far_east[CP:, :].astype(F32), 64, 1)
        cot_cols = jnp.where(lane_of((HID, PP)) < 64, far_west[CP:, :].astype(F32), cot_east)
        dcol = (cot_cols * slope).astype(BF16).astype(F32)
        moved = [dcol] + [pltpu.roll(dcol, PP - m, 1) for m in (1, 2)]
        side[...] = jnp.dot(
            backward_ref[...], jnp.concatenate(moved, axis=0).astype(BF16), preferred_element_type=F32
        )
        load(0).wait()

    for k in (1, 2, 3):

        @pl.when(step == 2 * k)
        def _():
            load(k).wait()

    @pl.when(step < 2)
    def _():
        finish_rows(forward_rows())
        next_rows()

    @pl.when((step >= 2) & (step <= ROWS // 2))
    def _():
        outs, terms = backward_rows()
        pres = forward_rows()
        finish_rows(pres)
        next_rows()
        store_backward(outs, terms)

    @pl.when(step == ROWS // 2 + 1)
    def _():
        store_backward(*backward_rows())

    for k in range(4):

        @pl.when(step == 2 * k + 2)
        def _():
            ship_act(k).start()

    @pl.when(step == ROWS // 2 + 1)
    def _():
        devices = packed.shape[0]
        per = TILE // slots
        tiles = packed.shape[1] // TILE
        ships = sem.shape[0]
        cut = -(-tiles // (2 * ships)) * 2
        pick = pick_ref[...]

        def ship(k):
            rows = pl.ds(k * cut * TILE, (min(tiles, (k + 1) * cut) - k * cut) * TILE)
            return pltpu.make_async_copy(packed.at[:, rows, :], reply_ref.at[:, rows, :], sem.at[k])

        started = []
        for t in range(0, tiles, 2):
            pair = [t, t + 1] if t + 1 < tiles else [t]
            data = []
            for u in pair:
                chans = [
                    dfield[pl.ds(min(u * per + p, CP - 1), PIECES, stride=CP), :].astype(BF16) for p in range(per)
                ]
                data.append(jnp.concatenate(chans, axis=0) if per > 1 else chans[0])
            data = jnp.concatenate(data, axis=1) if len(data) > 1 else data[0]
            got = jnp.dot(pick, data, preferred_element_type=F32).astype(BF16)
            for n, u in enumerate(pair):
                packed[:, u * TILE : (u + 1) * TILE, :] = got[:, n * PP : (n + 1) * PP].reshape(devices, TILE, PP)
            if (t + 2) % cut == 0 or t + 2 >= tiles:
                k = t // cut
                ship(k).start()
                started.append(k)
        for k in range(4):
            ship_act(k).wait()
        for k in started:
            ship(k).wait()


def conv_call(slots, part, field, top, bottom, own_west, own_east, far_west, far_east, cot, cot_top, cot_bottom, forward, backward, pick):
    devices = pick.shape[0] // TILE
    reply_rows = part - TILE
    edges = [whole(x.shape) for x in (field, top, bottom, own_west, own_east, far_west, far_east)]
    return pl.pallas_call(
        functools.partial(conv_kernel, slots),
        grid=(ROWS // 2 + 2,),
        in_specs=edges
        + [anywhere()]
        + [whole(x.shape) for x in (cot_top, cot_bottom, forward, backward, pick)],
        out_specs=[anywhere(), whole((GRAD_ROWS, HID)), anywhere()],
        out_shape=[
            jax.ShapeDtypeStruct((ROWS, HID, COLS), BF16),
            jax.ShapeDtypeStruct((GRAD_ROWS, HID), F32),
            jax.ShapeDtypeStruct((devices, reply_rows, PP), BF16),
        ],
        scratch_shapes=[
            pltpu.VMEM((ROWS + 6, CP, COLS), BF16),
            pltpu.VMEM((ROWS + 6, 3 * CP, COLS), BF16),
            pltpu.VMEM((ROWS + 2, HID, COLS), BF16),
            pltpu.VMEM((ROWS + 2, HID, COLS), BF16),
            pltpu.VMEM((ROWS + 2, HID, COLS), BF16),
            pltpu.VMEM((3 * CP, PP), F32),
            pltpu.VMEM((PIECES * CP, PP), F32),
            pltpu.VMEM((devices, reply_rows, PP), BF16),
            pltpu.SemaphoreType.DMA((4,)),
            pltpu.SemaphoreType.DMA((4,)),
            pltpu.SemaphoreType.DMA((4,)),
        ],
        compiler_params=params(),
        name="conv_level",
    )(field, top, bottom, own_west, own_east, far_west, far_east, cot, cot_top, cot_bottom, forward, backward, pick)


def return_kernel(slots, devices, place_ref, back_hbm, weight_hbm, out_ref, back, weights, back_f, out_f, back_sem, in_sem):
    blocks = out_ref.shape[1]
    chunks = in_sem.shape[0]
    group = blocks // chunks
    cuts = back_sem.shape[0]
    size = back.shape[0] // cuts
    share = devices // cuts
    rows = back.shape[0] // devices
    part = rows + TILE
    trash = devices * part

    def fetch(k):
        span = pl.ds(k * size, size)
        return pltpu.make_async_copy(back_hbm.at[span], back.at[span], back_sem.at[k])

    def load(k):
        rows = pl.ds(k * group, group)
        return pltpu.make_async_copy(weight_hbm.at[rows], weights.at[rows], in_sem.at[k])

    for k in range(cuts):
        fetch(k).start()
    for k in range(chunks):
        load(k).start()

    def widen(k, carry):
        fetch(k).wait()
        for i in range(share):
            at = pl.multiple_of((k * share + i) * rows, TILE)
            to = pl.multiple_of((k * share + i) * part, TILE)
            back_f[pl.ds(to, rows), :] = back[pl.ds(at, rows), :].astype(F32)
        return carry

    lax.fori_loop(0, cuts, widen, 0)
    back_f[pl.ds(trash, CP * slots), :] = jnp.zeros((CP * slots, PP), F32)

    def gradients(k, carry):
        load(k).wait()
        for i in range(group):
            b = k * group + i
            total = jnp.zeros((C, PP), F32)
            for half in range(2):
                got = []
                for part_j in range(2):
                    at = place_ref[b * K + 2 * half + part_j]
                    got.append(back_f[pl.ds(at, C, stride=slots), :].astype(BF16))
                pair = jnp.concatenate([weights[b, 2 * half], weights[b, 2 * half + 1]], axis=1)
                total = total + lax.dot_general(
                    jnp.concatenate(got, axis=1), pair, (((1,), (1,)), ((), ())), preferred_element_type=F32
                )
            out_f[pl.ds(b, C, stride=blocks), :] = total
        return carry

    lax.fori_loop(0, chunks, gradients, 0)
    for c in range(C):
        out_ref[c] = out_f[c * blocks : (c + 1) * blocks, :].astype(BF16)


def return_call(place, back, weights, devices, slots):
    blocks = weights.shape[0]
    return pl.pallas_call(
        functools.partial(return_kernel, slots, devices),
        grid=(1,),
        in_specs=[smem(), anywhere(), anywhere()],
        out_specs=whole((C, blocks, PP)),
        out_shape=jax.ShapeDtypeStruct((C, blocks, PP), BF16),
        scratch_shapes=[
            pltpu.VMEM(back.shape, BF16),
            pltpu.VMEM(weights.shape, BF16),
            pltpu.VMEM((back.shape[0] + devices * TILE + CP * slots, PP), F32),
            pltpu.VMEM((CP * blocks, PP), F32),
            pltpu.SemaphoreType.DMA((8,)),
            pltpu.SemaphoreType.DMA((2,)),
        ],
        compiler_params=params(),
        name="block_gradients",
    )(place, back, weights)


def shift(value, face_by, tile_by):
    faces, tiles = lax.axis_size("face"), lax.axis_size("tile")
    pairs = [
        (f * tiles + t, (f + face_by) % faces * tiles + t + tile_by)
        for f in range(faces)
        for t in range(tiles)
        if 0 <= t + tile_by < tiles
    ]
    return lax.ppermute(value, BOTH, pairs)


def swap(value, axis, bit):
    return lax.ppermute(value, axis, [(i, i ^ (1 << bit)) for i in range(lax.axis_size(axis))])


def upper(axis, bit):
    return (lax.axis_index(axis) >> bit) & 1


def fold(value, axis, bit):
    half = value.shape[0] // 2
    mine = upper(axis, bit)
    keep = lax.dynamic_slice_in_dim(value, mine * half, half, axis=0)
    send = lax.dynamic_slice_in_dim(value, (1 - mine) * half, half, axis=0)
    return keep + swap(send, axis, bit)


def unfold(value, axis, bit):
    got = swap(value, axis, bit)
    first = upper(axis, bit) == 0
    return jnp.concatenate([jnp.where(first, value, got), jnp.where(first, got, value)], axis=0)


def local(latlon, intersection_weight, target_dev, target_piece, counts, conv_weight, cotangent):
    faces, tiles = lax.axis_size("face"), lax.axis_size("tile")
    devices = faces * tiles
    blocks = latlon.shape[0]
    slots = max(2, (blocks * K + devices - 1) // devices)
    part = -(-C * slots // TILE) * TILE + TILE

    lat = jnp.swapaxes(latlon, 0, 1)
    send, place = send_call(
        target_dev.T, target_piece.T, counts, lat, intersection_weight, devices, slots, part
    )
    recv = lax.all_to_all(send.reshape(devices, part, PP), BOTH, split_axis=0, concat_axis=0, tiled=True)

    forward, backward = taps_call(jnp.swapaxes(conv_weight, 1, 2))
    cot = jnp.swapaxes(cotangent[0], 0, 1)
    cot_top = shift(cotangent[0, :, ROWS - 1, :], 0, 1)
    cot_bottom = shift(cotangent[0, :, 0, :], 0, -1)
    cot_west = jnp.pad(cotangent[0, :, :, 0], ((0, 0), (1, PP - ROWS - 1)))
    cot_east = jnp.pad(cotangent[0, :, :, COLS - 1], ((0, 0), (1, PP - ROWS - 1)))
    recv, forward, backward, cot, cot_west, cot_east = lax.optimization_barrier(
        (recv, forward, backward, cot, cot_west, cot_east)
    )

    field, low, high, west, east, pick = gather_call(recv, slots)
    top = shift(high, 0, 1)
    bottom = shift(low, 0, -1)
    west, east = columns_call(west, east, cot_west, cot_east, top, bottom, cot_top, cot_bottom)
    far_west = shift(east, 1, 0)
    far_east = shift(west, -1, 0)
    act, grad, reply = conv_call(
        slots, part, field, top, bottom, west, east, far_west, far_east, cot, cot_top, cot_bottom, forward, backward, pick
    )
    activation = with_layout_constraint(jnp.swapaxes(act, 0, 1), Layout((0, 1, 2)))

    back = lax.all_to_all(reply, BOTH, split_axis=0, concat_axis=0, tiled=True)

    halves = [("tile", 0)] + [("face", bit) for bit in range((faces - 1).bit_length())]
    grad = fold(grad, *halves[0])
    grad, activation = lax.optimization_barrier((grad, activation))
    for axis, bit in halves[1:]:
        grad = fold(grad, axis, bit)
    groups = [list(range(first, tiles, 2)) for first in range(2)]
    grad = lax.psum(grad, "tile", axis_index_groups=groups)
    grad = grad * (1.0 / math.sqrt(devices * ROWS * COLS))
    for axis, bit in reversed(halves):
        grad = unfold(grad, axis, bit)
    grad_conv = jnp.swapaxes(grad[: 9 * CP].reshape(9, CP, HID)[:, :C, :], 1, 2)

    back = back.reshape(devices * (part - TILE), PP)
    grad_lat = return_call(place, back, intersection_weight, devices, slots)
    return (activation[None], grad_conv, jnp.swapaxes(grad_lat, 0, 1))


def solution(mesh):
    placed = (
        P(BOTH, None, None),
        P(BOTH, None, None, None),
        P(BOTH, None),
        P(BOTH, None),
        P(BOTH),
        P(),
        P("face", None, "tile", None),
    )
    return jax.shard_map(
        local,
        mesh=mesh,
        in_specs=placed,
        out_specs=(P("face", None, "tile", None), P(), P(BOTH, None, None)),
        check_vma=False,
    )
```
